512 devices in a mesh: ty: 16 (over z, core), tx: 32 (over y, x).
Axes of the slice: x: 4, y: 8, z: 8, core: 2. Of those that a mesh axis runs over, the one named last changes fastest.
Arguments:
- excite_l0: float32 [16, 32, 1024], P(None, 'ty', 'tx'), may hold values from -6 to 6
- excite_l1: float32 [16, 64, 2048], P(None, 'ty', 'tx'), may hold values from -6 to 6
- excite_l2: float32 [16, 128, 4096], P(None, 'ty', 'tx'), may hold values from -6 to 6
- excite_l3: float32 [16, 256, 8192], P(None, 'ty', 'tx'), may hold values from -6 to 6
- refine_weights: float32 [3, 4, 9], replicated, may hold values from -2 to 2
- block_factor: float32 [3, 4, 4], replicated, may hold values from -3 to 3
- channel_factor: float32 [16, 16], replicated, may hold values from -1.5 to 1.5
- cotangent: float32 [16, 256, 8192], P(None, 'ty', 'tx'), may hold values from -6 to 6
Outputs:
- sky: float32 [16, 256, 8192], P(None, 'ty', 'tx')
- grad_l0: float32 [16, 32, 1024], P(None, 'ty', 'tx')
- grad_l1: float32 [16, 64, 2048], P(None, 'ty', 'tx')
- grad_l2: float32 [16, 128, 4096], P(None, 'ty', 'tx')
- grad_l3: float32 [16, 256, 8192], P(None, 'ty', 'tx')
The draws below stay inside these ranges and needn't reach their ends.
All inputs are finite; a program needn't handle non-finite values.
Results may differ from the reference program's by a relative error of at most 0.00013.
Values sent between devices are 32-bit elements; how exact they have to be, the bound alone decides.
No kernel may reach another device: no remote copies, remote signals or barrier semaphores. Data moves between devices by JAX's collectives and lax.ppermute only.
A program may use at most 64 MiB of HBM per device.

```python
import jax
import jax.numpy as jnp
from jax import lax

C = 16
LEVELS = 4
ROWS_L3 = 256
COLS_L3 = 8192
ROWS_L2 = 128
COLS_L2 = 4096
ROWS_L1 = 64
COLS_L1 = 2048
ROWS_L0 = 32
COLS_L0 = 1024


def steps_of(own_key, dims, split, least, top_value):
    loudness, own = 1.0, jax.random.fold_in(own_key, 6)
    for position, parts in split:
        draws = jnp.exp(jax.random.uniform(jax.random.fold_in(own, position), (parts,), jnp.float32, least / len(split), top_value / len(split)))
        loudness = loudness * jnp.repeat(draws, dims[position] // parts).reshape([-1 if axis == position else 1 for axis in range(len(dims))])
    return loudness


def noise(rng, extent, scale, bound, pieces=(), kind=jnp.bfloat16):
    array = jax.random.normal(rng, extent, jnp.float32) * scale
    if len(pieces) > 0:
        array = steps_of(rng, extent, pieces, -0.22, 0.18) * array
    return jnp.clip(array, min=-bound, max=bound).astype(kind)


def setup_inputs(seed: int = 0) -> dict:
    key_list = jax.random.split(jax.random.key(seed), 9)
    return {
        "excite_l0": noise(key_list[0], (C, ROWS_L0, COLS_L0), 1.0, 6.0, ((1, 16), (2, 32)), jnp.float32),
        "excite_l1": noise(key_list[1], (C, ROWS_L1, COLS_L1), 1.0, 6.0, ((1, 16), (2, 32)), jnp.float32),
        "excite_l2": noise(key_list[2], (C, ROWS_L2, COLS_L2), 1.0, 6.0, ((1, 16), (2, 32)), jnp.float32),
        "excite_l3": noise(key_list[3], (C, ROWS_L3, COLS_L3), 1.0, 6.0, ((1, 16), (2, 32)), jnp.float32),
        "refine_weights": noise(key_list[4], (LEVELS - 1, 4, 9), 9 ** -0.5, 2.0, (), jnp.float32),
        "block_factor": noise(key_list[5], (LEVELS - 1, 4, 4), 4 ** -0.5, 3.0, (), jnp.float32),
        "channel_factor": noise(key_list[6], (C, C), C ** -0.5, 1.5, (), jnp.float32),
        "cotangent": noise(key_list[7], (C, ROWS_L3, COLS_L3), 1.0, 6.0, ((1, 16), (2, 32)), jnp.float32),
    }


def mix_channels(factor, field):
    return jnp.einsum('cd,dij->cij', factor, field, precision=lax.Precision.HIGHEST)

def refine_level(padded, mixed, rmat, dmat):
    chans = padded.shape[0]
    rows = padded.shape[1] - 2
    cols = padded.shape[2] - 2
    views = jnp.stack([padded[:, 1 + da:1 + da + rows, 1 + db:1 + db + cols] for da in (-1, 0, 1) for db in (-1, 0, 1)])
    blocks = mixed.reshape(chans, rows, 2, cols, 2).transpose(2, 4, 0, 1, 3).reshape(4, chans, rows, cols)
    finer = jnp.einsum('kn,ncij->kcij', rmat, views, precision=lax.Precision.HIGHEST)
    finer = finer + jnp.einsum('km,mcij->kcij', dmat, blocks, precision=lax.Precision.HIGHEST)
    return finer.reshape(2, 2, chans, rows, cols).transpose(2, 3, 0, 4, 1).reshape(chans, 2 * rows, 2 * cols)

def reference(excite_l0, excite_l1, excite_l2, excite_l3, refine_weights, block_factor, channel_factor, cotangent):

    def forward(exc0, exc1, exc2, exc3):
        excites = [exc0, exc1, exc2, exc3]
        field = mix_channels(channel_factor, excites[0])
        for level in range(1, 4):
            padded = jnp.pad(field, ((0, 0), (1, 1), (1, 1)))
            field = refine_level(padded, mix_channels(channel_factor, excites[level]), refine_weights[level - 1], block_factor[level - 1])
        return field
    sky, pullback = jax.vjp(forward, excite_l0, excite_l1, excite_l2, excite_l3)
    grads = pullback(cotangent)
    return (sky, grads[0], grads[1], grads[2], grads[3])
```

```python
import jax
import jax.numpy as jnp
from jax import lax
from jax.experimental import pallas as pl
from jax.experimental.pallas import tpu as pltpu
from jax.sharding import PartitionSpec as P

F32 = jnp.float32
CH = 16
COLS = (32, 64, 128, 256)
ROWS = (2, 4, 8, 16)
WIDE = (128, 128, 256, 256)
VMEM_LIMIT = 40 * 1024 * 1024


def iota(shape, dim):
    return lax.broadcasted_iota(jnp.int32, shape, dim)


def mul(left, right):
    return lax.dot_general(
        left, right, (((1,), (0,)), ((), ())),
        precision=lax.Precision.HIGHEST, preferred_element_type=F32,
    )


def mul_t(left, right):
    return lax.dot_general(
        left, right, (((1,), (1,)), ((), ())),
        precision=lax.Precision.HIGHEST, preferred_element_type=F32,
    )


def col_of(lane, cols, none):
    return jnp.where(
        lane < cols,
        lane,
        jnp.where(lane < cols + 2, lane - cols - 2, jnp.where(lane < cols + 4, lane - 2, none)),
    )


def refine_matrix(weights, level):
    fine, coarse = WIDE[level], WIDE[level - 1]
    fine_col = col_of(iota((fine // 8, 8, coarse), 0) * 8 + iota((fine // 8, 8, coarse), 1), COLS[level], -4096)
    coarse_col = col_of(iota((fine // 8, 8, coarse), 2), COLS[level - 1], 4096)
    step = coarse_col - (fine_col >> 1)
    odd = iota((1, 8, coarse), 1) & 1
    bands = []
    for a in (0, 1):
        parts = []
        for da in (0, 1, 2):
            block = jnp.zeros((fine // 8, 8, coarse), F32)
            for db in (0, 1, 2):
                n = 3 * da + db
                pair = jnp.where(odd == 0, weights[level - 1, 2 * a, n], weights[level - 1, 2 * a + 1, n])
                block = jnp.where(step == db - 1, pair, block)
            parts.append(block.reshape(fine, coarse))
        bands.append(jnp.concatenate(parts, axis=1))
    return jnp.concatenate(bands, axis=0)


def push(rows, matrix, level):
    blocks = len(rows) - 2
    left = jnp.concatenate(
        [jnp.concatenate(rows[da : da + blocks], axis=0) for da in (0, 1, 2)], axis=1
    )
    return mul_t(left, matrix)


def push_rows(rows, matrix, level):
    fine = WIDE[level]
    out = push(rows, matrix, level)
    result = []
    for i in range(len(rows) - 2):
        for a in (0, 1):
            result.append(out[CH * i : CH * (i + 1), fine * a : fine * (a + 1)])
    return result


def pull(left, matrix, level, blocks):
    coarse = WIDE[level - 1]
    out = mul(left, matrix)
    result = []
    for i in range(-1, blocks + 1):
        total = None
        for da in (0, 1, 2):
            block = i - (da - 1)
            if 0 <= block < blocks:
                term = out[CH * block : CH * (block + 1), coarse * da : coarse * (da + 1)]
                total = term if total is None else total + term
        result.append(total)
    return result


def pull_rows(rows, matrix, level):
    blocks = len(rows) // 2
    left = jnp.concatenate(
        [jnp.concatenate([rows[2 * i + a] for i in range(blocks)], axis=0) for a in (0, 1)], axis=1
    )
    return pull(left, matrix, level, blocks)


def swap_lanes(x):
    axis = x.ndim - 1
    lane = iota(x.shape, axis)
    return jnp.where((lane & 1) == 0, pltpu.roll(x, x.shape[axis] - 1, axis), pltpu.roll(x, 1, axis))


def factor_rows(rows, factor, level, transposed):
    odd = iota(rows[0].shape, 1) & 1
    swapped = [swap_lanes(r) for r in rows]

    def entry(a, b, a2, b2):
        if transposed:
            return factor[level - 1, 2 * a2 + b2, 2 * a + b]
        return factor[level - 1, 2 * a + b, 2 * a2 + b2]

    result = []
    for i in range(len(rows) // 2):
        for a in (0, 1):
            total = None
            for a2 in (0, 1):
                same = jnp.where(odd == 0, entry(a, 0, a2, 0), entry(a, 1, a2, 1))
                other = jnp.where(odd == 0, entry(a, 0, a2, 1), entry(a, 1, a2, 0))
                term = same * rows[2 * i + a2] + other * swapped[2 * i + a2]
                total = term if total is None else total + term
            result.append(total)
    return result


def factor_tile(x, factor, transposed):
    odd_row = iota((1, 8, 128), 1) & 1
    odd_col = iota((1, 8, 128), 2) & 1
    side = swap_lanes(x)

    def swap_rows(y):
        row = iota(y.shape, 1)
        return jnp.where((row & 1) == 0, pltpu.roll(y, 7, 1), pltpu.roll(y, 1, 1))

    def coefficient(flip_row, flip_col):
        values = []
        for a in (0, 1):
            for b in (0, 1):
                here, there = 2 * a + b, 2 * (a ^ flip_row) + (b ^ flip_col)
                values.append(factor[2, there, here] if transposed else factor[2, here, there])
        return jnp.where(
            odd_row == 0,
            jnp.where(odd_col == 0, values[0], values[1]),
            jnp.where(odd_col == 0, values[2], values[3]),
        )

    return (
        coefficient(0, 0) * x
        + coefficient(0, 1) * side
        + coefficient(1, 0) * swap_rows(x)
        + coefficient(1, 1) * swap_rows(side)
    )


def spread_factor(mixing):
    return mul(jnp.where(iota((256, CH), 0) // CH == iota((256, CH), 1), 1.0, 0.0), mixing)


def mix_sorted(mixing):
    spread = spread_factor(mixing)
    tiled = jnp.where((iota((256, CH), 0) & 15) == iota((256, CH), 1), 1.0, 0.0)
    full = mul_t(spread, tiled)
    row = iota((256, 256), 0) & 15
    col = iota((256, 256), 1)
    return jnp.where(row == 2 * ((col & 127) >> 4) + (col >> 7), full, 0.0)


def mix_sorted_t(mixing):
    spread = spread_factor(mixing)
    tiled = jnp.where((iota((256, CH), 0) & 15) == iota((256, CH), 1), 1.0, 0.0)
    full = mul_t(tiled, spread)
    col = iota((256, 256), 1) & 15
    row = iota((256, 256), 0)
    return jnp.where(col == 2 * ((row & 127) >> 4) + (row >> 7), full, 0.0)


def edge_mask(width, cols, at_left, at_right):
    lane = iota((1, width), 1)
    left = jnp.where((lane >= cols) & (lane < cols + 2), at_left, 0)
    right = jnp.where((lane >= cols + 2) & (lane < cols + 4), at_right, 0)
    return jnp.where(left + right > 0, 0.0, 1.0)


def clear_outside(rows, before, after, place, grid, level, width):
    ty, tx = place
    cols = edge_mask(
        width, COLS[level], (tx == 0).astype(jnp.int32), (tx == grid[1] - 1).astype(jnp.int32)
    )
    top = jnp.where(ty == 0, 0.0, 1.0)
    bottom = jnp.where(ty == grid[0] - 1, 0.0, 1.0)
    result = []
    for k, row in enumerate(rows):
        mask = cols
        if k < before:
            mask = cols * top
        elif k >= len(rows) - after:
            mask = cols * bottom
        result.append(row * mask)
    return result


def wide(x, width):
    if x.shape[1] == width:
        return x
    return jnp.concatenate([x, jnp.zeros((x.shape[0], width - x.shape[1]), F32)], axis=1)


def move(x, source, target, lane):
    shift = (target - source) % 128
    moved = pltpu.roll(x, shift, 1) if shift else x
    return jnp.where((lane >= target) & (lane < target + 2), moved, 0.0)


def gather_lanes(pieces, lane):
    total = jnp.zeros((CH, 128), F32)
    for k, (x, source) in enumerate(pieces):
        shift = (2 * k - source) % 128
        moved = pltpu.roll(x, shift, 1) if shift else x
        total = jnp.where((lane >= 2 * k) & (lane < 2 * k + 2), moved, total)
    return total


def halo_tile(x, level):
    return x[:, 128:] if level == 2 else x


def first_kernel(grid):
    def body(weights, factor, place_ref, mixing, cot, e0, e1, e2, send_a, send_b, g0, g1, g2, u0, u1, u2):
        place = (place_ref[0], place_ref[1])
        lane = iota((CH, 128), 1)
        pixels = mul(mix_sorted_t(mixing[...]), cot[...].reshape(256, 256))
        left = jnp.concatenate([pixels[:128], pixels[128:]], axis=1)
        ups = [None, None, None]
        ups[2] = pull(left, refine_matrix(weights, 3), 3, 8)
        ups[2] = clear_outside(ups[2], 1, 1, place, grid, 2, 256)
        none = jnp.zeros((CH, 256), F32)
        ups[1] = pull_rows([none] + ups[2] + [none], refine_matrix(weights, 2), 2)
        ups[1] = clear_outside(ups[1], 2, 2, place, grid, 1, 128)
        ups[0] = pull_rows(ups[1], refine_matrix(weights, 1), 1)
        gs = [[wide(e0[:, r, :], 128) for r in range(2)]]
        gs.append(factor_rows([wide(e1[:, r, :], 128) for r in range(4)], factor, 1, False))
        gs.append(factor_rows([e2[:, r, :] for r in range(8)], factor, 2, False))
        high, low = [], []
        for level in (0, 1, 2):
            for row in gs[level]:
                high.append((row, COLS[level] - 2))
                low.append((row, 0))
        for level in (0, 1, 2):
            base = COLS[level] % 128
            for row in ups[level]:
                high.append((halo_tile(row, level), base + 2))
                low.append((halo_tile(row, level), base))
        high, low = gather_lanes(high, lane), gather_lanes(low, lane)
        even = (place[1] & 1) == 0
        send_a[...] = jnp.where(even, high, low)
        send_b[...] = jnp.where(even, low, high)
        for ref, rows in ((g0, gs[0]), (g1, gs[1]), (g2, gs[2]), (u0, ups[0]), (u1, ups[1]), (u2, ups[2])):
            for k, row in enumerate(rows):
                ref[k] = row[:, :128]

    return body


def second_kernel(grid):
    def body(place_ref, got_a, got_b, g0, g1, g2, u0, u1, u2, send_a, send_b, x0, x1, x2, v0, v1, v2):
        ty, tx = place_ref[0], place_ref[1]
        lane = iota((CH, 128), 1)
        even = (tx & 1) == 0
        from_right = jnp.where(even, got_a[...], got_b[...])
        from_left = jnp.where(even, got_b[...], got_a[...])
        k = 0
        wides, ups = [], []
        for level, ref in ((0, g0), (1, g1), (2, g2)):
            rows = []
            for r in range(ROWS[level]):
                base = COLS[level] % 128
                halo = move(from_left, 2 * k, base, lane) + move(from_right, 2 * k, base + 2, lane)
                rows.append([ref[r], halo] if level == 2 else [ref[r] + halo])
                k += 1
            wides.append(rows)
        for level, ref in ((0, u0), (1, u1), (2, u2)):
            rows = []
            for r in range(ref.shape[0]):
                rows.append(
                    ref[r] + move(from_left, 2 * k, 0, lane) + move(from_right, 2 * k, COLS[level] - 2, lane)
                )
                k += 1
            ups.append(rows)
        low = [t for level in (0, 1, 2) for row in wides[level][:2] for t in row]
        high = [t for level in (0, 1, 2) for row in wides[level][-2:] for t in row]
        low += ups[0][:2] + ups[1][:2] + ups[2][:1]
        high += ups[0][-2:] + ups[1][-2:] + ups[2][-1:]
        even = (ty & 1) == 0
        for j in range(len(low)):
            send_a[j] = jnp.where(even, high[j], low[j])
            send_b[j] = jnp.where(even, low[j], high[j])
        for ref, rows in ((x0, wides[0]), (x1, wides[1]), (x2, wides[2])):
            for j, row in enumerate(rows):
                ref[j] = row[0] if len(row) == 1 else jnp.concatenate(row, axis=1)
        for ref, rows, trim in ((v0, ups[0], 2), (v1, ups[1], 2), (v2, ups[2], 1)):
            for j in range(ref.shape[0]):
                ref[j] = rows[j + trim]

    return body


def third_kernel(grid):
    def body(weights, factor, place_ref, mixing, got_a, got_b, x0, x1, x2, v0, v1, v2, local, sky, d0, d1, d2):
        place = (place_ref[0], place_ref[1])
        even = (place[0] & 1) == 0

        def pick(j):
            first, second = got_a[j], got_b[j]
            return jnp.where(even, second, first), jnp.where(even, first, second)

        tiles = [pick(j) for j in range(13)]
        above, below = [t[0] for t in tiles], [t[1] for t in tiles]

        def join(parts):
            return [jnp.concatenate(parts[0:2], axis=1), jnp.concatenate(parts[2:4], axis=1)]

        field = above[0:2] + [x0[r] for r in range(2)] + below[0:2]
        mixed = above[2:4] + [x1[r] for r in range(4)] + below[2:4]
        field = push_rows(field, refine_matrix(weights, 1), 1)
        field = [f + m for f, m in zip(field, mixed)]
        field = clear_outside(field, 2, 2, place, grid, 1, 128)
        mixed = join(above[4:8]) + [x2[r] for r in range(8)] + join(below[4:8])
        field = push_rows(field, refine_matrix(weights, 2), 2)
        field = [f + m for f, m in zip(field, mixed)]
        field = clear_outside(field, 2, 2, place, grid, 2, 256)
        fine = push(field[1:11], refine_matrix(weights, 3), 3)
        fine = jnp.concatenate([fine[:, :256], fine[:, 256:]], axis=0)
        sky[...] = (mul(mix_sorted(mixing[...]), fine) + local[...]).reshape(CH, 16, 256)
        up0 = [v0[r] + above[8 + r] + below[8 + r] for r in range(2)]
        up1 = [v1[r] for r in range(4)]
        up1 = [up1[0] + above[10], up1[1] + above[11], up1[2] + below[10], up1[3] + below[11]]
        up2 = [v2[r] for r in range(8)]
        up2[0] = up2[0] + above[12]
        up2[7] = up2[7] + below[12]
        up1 = factor_rows(up1, factor, 1, True)
        up2 = factor_rows(up2, factor, 2, True)
        for ref, rows, cols in ((d0, up0, 32), (d1, up1, 64), (d2, up2, 128)):
            for r, row in enumerate(rows):
                ref[:, r, :] = row[:, :cols]

    return body


def local_body(factor, mixing, cot, e3, local, grad):
    spread = spread_factor(mixing[...])
    column = jnp.where(iota((256, CH), 0) // CH == iota((256, CH), 1), 1.0, 0.0)
    same = (iota((256, 256), 0) & 15) == (iota((256, 256), 1) & 15)

    def factored(ref, transposed):
        halves = [
            factor_tile(ref[:, :, 128 * h : 128 * (h + 1)].reshape(32, 8, 128), factor, transposed).reshape(256, 128)
            for h in (0, 1)
        ]
        return jnp.concatenate(halves, axis=1)

    grad[...] = mul(jnp.where(same, mul_t(column, spread), 0.0), factored(cot, True)).reshape(CH, 16, 256)
    local[...] = mul(jnp.where(same, mul_t(spread, column), 0.0), factored(e3, False))


def swaps(count, first):
    pairs = []
    for i in range(first, count - 1, 2):
        pairs += [(i, i + 1), (i + 1, i)]
    return pairs


def shaped(*shape):
    return jax.ShapeDtypeStruct(shape, F32)


SMEM = pl.BlockSpec(memory_space=pltpu.SMEM)
VMEM = pl.BlockSpec(memory_space=pltpu.VMEM)


def call(body, specs, outs, args):
    return pl.pallas_call(
        body,
        out_shape=outs,
        in_specs=specs,
        out_specs=[VMEM] * len(outs),
        compiler_params=pltpu.CompilerParams(vmem_limit_bytes=VMEM_LIMIT),
    )(*args)


def device_body(grid):
    def on_device(e0, e1, e2, e3, weights, factor, mixing, cot):
        place = jnp.stack([lax.axis_index("ty"), lax.axis_index("tx")]).astype(jnp.int32)
        rows = [shaped(2, CH, 128), shaped(4, CH, 128), shaped(8, CH, 128)]
        ups = [shaped(6, CH, 128), shaped(8, CH, 128), shaped(10, CH, 128)]
        first = call(
            first_kernel(grid),
            [SMEM] * 3 + [VMEM] * 5,
            [shaped(CH, 128)] * 2 + rows + ups,
            (weights, factor, place, mixing, cot, e0, e1, e2),
        )
        got_a = lax.ppermute(first[0], "tx", swaps(grid[1], 0))
        got_b = lax.ppermute(first[1], "tx", swaps(grid[1], 1))
        second = call(
            second_kernel(grid),
            [SMEM] + [VMEM] * 8,
            [shaped(13, CH, 128)] * 2 + [shaped(2, CH, 128), shaped(4, CH, 128), shaped(8, CH, 256)] + rows,
            (place, got_a, got_b, *first[2:]),
        )
        local, grad3 = call(
            local_body,
            [SMEM] + [VMEM] * 3,
            [shaped(256, 256), shaped(CH, 16, 256)],
            (factor, mixing, cot, e3),
        )
        got_a = lax.ppermute(second[0], "ty", swaps(grid[0], 0))
        got_b = lax.ppermute(second[1], "ty", swaps(grid[0], 1))
        sky, grad0, grad1, grad2 = call(
            third_kernel(grid),
            [SMEM] * 3 + [VMEM] * 10,
            [shaped(CH, 16, 256), shaped(CH, 2, 32), shaped(CH, 4, 64), shaped(CH, 8, 128)],
            (weights, factor, place, mixing, got_a, got_b, *second[2:], local),
        )
        return (sky, grad0, grad1, grad2, grad3)

    return on_device


def solution(mesh):
    tiles = P(None, "ty", "tx")
    return jax.shard_map(
        device_body((mesh.shape["ty"], mesh.shape["tx"])),
        mesh=mesh,
        in_specs=(tiles, tiles, tiles, tiles, P(), P(), P(), tiles),
        out_specs=(tiles,) * 5,
        check_vma=False,
    )
```

```python
import jax
import jax.numpy as jnp
from jax import lax
from jax.experimental import pallas as pl
from jax.experimental.pallas import tpu as pltpu
from jax.sharding import PartitionSpec as P

F32 = jnp.float32
BF16 = jnp.bfloat16
CH = 16
COLS = (32, 64, 128, 256)
ROWS = (2, 4, 8, 16)
BASE = (64, 0, 0, 0)
HALO = (96, 100, 104)
VMEM_LIMIT = 40 * 1024 * 1024


def iota(shape, dim):
    return lax.broadcasted_iota(jnp.int32, shape, dim)


def dot(left, right, dims, precision=None):
    return lax.dot_general(
        left, right, (dims, ((), ())), precision=precision, preferred_element_type=F32
    )


NN = ((1,), (0,))
NT = ((1,), (1,))


def mul(left, right):
    return dot(left, right, NN, lax.Precision.HIGHEST)


def mul_t(left, right):
    return dot(left, right, NT, lax.Precision.HIGHEST)


def split(x):
    high = x.astype(BF16)
    return high, (x - high.astype(F32)).astype(BF16)


def mul3(left, right, dims):
    return (
        dot(left[0], right[0], dims) + (dot(left[1], right[0], dims) + dot(left[0], right[1], dims))
    )


def roll(x, shift):
    shift %= 128
    return pltpu.roll(x, shift, 1) if shift else x


def places():
    return lax.axis_index("ty"), lax.axis_index("tx")


def refine_weight(weights, level, fine_col, coarse_col, a, da):
    step = coarse_col - (fine_col >> 1)
    odd = iota((1, 8, coarse_col.shape[2]), 1) & 1
    block = jnp.zeros(step.shape, F32)
    for db in (0, 1, 2):
        n = 3 * da + db
        pair = jnp.where(odd == 0, weights[level - 1, 2 * a, n], weights[level - 1, 2 * a + 1, n])
        block = jnp.where(step == db - 1, pair, block)
    return block.reshape(step.shape[0] * 8, step.shape[2])


def fine_index(count):
    shape = (count // 8, 8, 128)
    return iota(shape, 0) * 8 + iota(shape, 1)


def lane_index(count):
    return iota((count // 8, 8, 128), 2)


def interior_col(lane, level, none):
    cols, base = COLS[level], BASE[level]
    return jnp.where((lane >= base) & (lane < base + cols), lane - base, none)


def halo_col(lane, level, place, none):
    step = lane - place
    return jnp.where(
        (step >= 0) & (step < 4), jnp.where(step < 2, step - 2, step - 2 + COLS[level]), none
    )


def both_col(lane, level, none):
    return interior_col(lane, level, halo_col(lane, level, HALO[level], none))


FAR, NEAR = -4096, 4096


def matrix_1(weights):
    fine, coarse = fine_index(128), lane_index(128)
    fine, coarse = both_col(fine, 1, FAR), both_col(coarse, 0, NEAR)
    return [[refine_weight(weights, 1, fine, coarse, a, da) for da in (0, 1, 2)] for a in (0, 1)]


def matrix_2(weights):
    index, coarse = fine_index(128), both_col(lane_index(128), 1, NEAR)
    inner = interior_col(index, 2, FAR)
    rows = [[refine_weight(weights, 2, inner, coarse, a, da) for da in (0, 1, 2)] for a in (0, 1)]
    halos = [halo_col(index, 2, HALO[2] + 4 * a, FAR) for a in (0, 1)]
    rows.append(
        [sum(refine_weight(weights, 2, halos[a], coarse, a, da) for a in (0, 1)) for da in (0, 1, 2)]
    )
    return rows


def matrix_3(weights):
    index, lane = fine_index(256), lane_index(256)
    inner = interior_col(lane, 2, NEAR)
    halos = [halo_col(lane, 2, HALO[2] + 4 * da, NEAR) for da in (0, 1, 2)]
    rows = []
    for a in (0, 1):
        row = [refine_weight(weights, 3, index, inner, a, da) for da in (0, 1, 2)]
        row.append(sum(refine_weight(weights, 3, index, halos[da], a, da) for da in (0, 1, 2)))
        rows.append(row)
    return rows


def store_matrix(blocks, high_ref, low_ref):
    down = 0
    for row in blocks:
        for j, block in enumerate(row):
            high, low = split(block)
            high_ref[down : down + block.shape[0], 128 * j : 128 * (j + 1)] = high
            low_ref[down : down + block.shape[0], 128 * j : 128 * (j + 1)] = low
        down += row[0].shape[0]


def stack(rows):
    return jnp.concatenate(rows, axis=0)


def beside(parts):
    return jnp.concatenate(parts, axis=1)


def block_sum(out, blocks, part):
    result = []
    for i in range(-1, blocks + 1):
        total = None
        for da in (0, 1, 2):
            block = i - (da - 1)
            if 0 <= block < blocks:
                term = part(out[CH * block : CH * (block + 1)], da)
                total = term if total is None else total + term
        result.append(total)
    return result


def tile(x, j):
    return x[:, 128 * j : 128 * (j + 1)]


def swap_lanes(x):
    axis = x.ndim - 1
    lane = iota(x.shape, axis)
    return jnp.where((lane & 1) == 0, pltpu.roll(x, x.shape[axis] - 1, axis), pltpu.roll(x, 1, axis))


def factor_rows(rows, factor, level, transposed):
    odd = iota(rows[0].shape, 1) & 1
    swapped = [swap_lanes(r) for r in rows]

    def entry(a, b, a2, b2):
        if transposed:
            return factor[level - 1, 2 * a2 + b2, 2 * a + b]
        return factor[level - 1, 2 * a + b, 2 * a2 + b2]

    pairs = {}
    for a in (0, 1):
        for a2 in (0, 1):
            pairs[a, a2] = (
                jnp.where(odd == 0, entry(a, 0, a2, 0), entry(a, 1, a2, 1)),
                jnp.where(odd == 0, entry(a, 0, a2, 1), entry(a, 1, a2, 0)),
            )
    result = []
    for i in range(len(rows) // 2):
        for a in (0, 1):
            total = None
            for a2 in (0, 1):
                same, other = pairs[a, a2]
                term = same * rows[2 * i + a2] + other * swapped[2 * i + a2]
                total = term if total is None else total + term
            result.append(total)
    return result


def factor_tile(x, factor, transposed):
    odd_row = iota((1, 8, 128), 1) & 1
    odd_col = iota((1, 8, 128), 2) & 1
    side = swap_lanes(x)

    def swap_rows(y):
        row = iota(y.shape, 1)
        return jnp.where((row & 1) == 0, pltpu.roll(y, 7, 1), pltpu.roll(y, 1, 1))

    def coefficient(flip_row, flip_col):
        values = []
        for a in (0, 1):
            for b in (0, 1):
                here, there = 2 * a + b, 2 * (a ^ flip_row) + (b ^ flip_col)
                values.append(factor[2, there, here] if transposed else factor[2, here, there])
        return jnp.where(
            odd_row == 0,
            jnp.where(odd_col == 0, values[0], values[1]),
            jnp.where(odd_col == 0, values[2], values[3]),
        )

    return (
        coefficient(0, 0) * x
        + coefficient(0, 1) * side
        + coefficient(1, 0) * swap_rows(x)
        + coefficient(1, 1) * swap_rows(side)
    )


def inside_mask(place, tx, last, keep_rest):
    lane = iota((1, 128), 1) - place
    left = jnp.where(tx == 0, 0.0, 1.0)
    right = jnp.where(tx == last, 0.0, 1.0)
    rest = jnp.full((1, 128), 1.0 if keep_rest else 0.0, F32)
    return jnp.where((lane >= 0) & (lane < 2), left, jnp.where((lane >= 2) & (lane < 4), right, rest))


def clear_outside(rows, around, mask, ty, last):
    top = jnp.where(ty == 0, 0.0, 1.0)
    bottom = jnp.where(ty == last, 0.0, 1.0)
    result = []
    for k, row in enumerate(rows):
        if k < around:
            row = row * (mask * top)
        elif k >= len(rows) - around:
            row = row * (mask * bottom)
        else:
            row = row * mask
        result.append(row)
    return result


def edge_col(lane, level, none):
    inside = (0, 2, 6, 16)[level]
    cols = COLS[level]
    if level == 3:
        return jnp.where(lane < 16, lane, jnp.where(lane < 32, cols + lane - 32, none))
    col = jnp.where(lane < 2, lane - 2, jnp.where(lane < 4, cols + lane - 2, none))
    col = jnp.where((lane >= 4) & (lane < 4 + inside), lane - 4, col)
    return jnp.where(
        (lane >= 4 + inside) & (lane < 4 + 2 * inside), cols - inside + lane - 4 - inside, col
    )


def edge_pull(rows, weights, level, width):
    blocks = len(rows) // 2
    fine = edge_col(fine_index(width), level, FAR)
    coarse = edge_col(lane_index(width), level - 1, NEAR)
    parts = []
    for da in (0, 1, 2):
        total = None
        for a in (0, 1):
            left = stack([rows[2 * i + a] for i in range(blocks)])[:, :width]
            term = mul(left, refine_weight(weights, level, fine, coarse, a, da))
            total = term if total is None else total + term
        parts.append(total)
    return block_sum(beside(parts), blocks, tile)


def widen(x):
    if x.shape[1] == 128:
        return x
    return beside([x, jnp.zeros((x.shape[0], 128 - x.shape[1]), F32)])


def first_kernel(grid):
    def body(weights_in, factor_in, cot_in, e0_in, e1_in, e2_in, send, weights, factor, cot, e0, e1, e2, edge, sems):
        copies = [
            pltpu.make_async_copy(source, target, sems.at[k])
            for k, (source, target) in enumerate(
                ((cot_in, cot), (weights_in, weights), (factor_in, factor), (e0_in, e0), (e1_in, e1), (e2_in, e2))
            )
        ]
        for copy in copies:
            copy.start()
        ty, tx = places()
        lane = iota((CH, 128), 1)
        for copy in copies[2:]:
            copy.wait()

        def edges(row, level):
            return jnp.where(lane < 2, row, roll(row, 4 - COLS[level]))

        pieces = [edges(widen(e0[:, r, :]), 0) for r in range(2)]
        pieces += factor_rows([edges(widen(e1[:, r, :]), 1) for r in range(4)], factor, 1, False)
        pieces += factor_rows([edges(e2[:, r, :], 2) for r in range(8)], factor, 2, False)
        for copy in copies[:2]:
            copy.wait()
        low = cot[:, :, :128].reshape(256, 128)
        high = cot[:, :, 128:].reshape(256, 128)
        edge[...] = jnp.where(iota((256, 128), 1) < 16, low, roll(high, 32))
        rows = [edge[pl.ds(r, CH, stride=16), :] for r in range(16)]
        mask = inside_mask(0, tx, grid[1] - 1, True)
        up2 = clear_outside(edge_pull(rows, weights, 3, 32), 1, mask, ty, grid[0] - 1)
        none = jnp.zeros((CH, 128), F32)
        up1 = edge_pull([none] + up2 + [none], weights, 2, 16)
        up1 = clear_outside(up1, 2, mask, ty, grid[0] - 1)
        up0 = edge_pull(up1, weights, 1, 8)
        pieces += up0 + up1 + up2
        totals = [none, none]
        for k, piece in enumerate(pieces):
            at = 4 * (k % 32)
            totals[k // 32] = jnp.where((lane >= at) & (lane < at + 4), roll(piece, at), totals[k // 32])
        send[0] = totals[0]
        send[1] = totals[1]

    return body


def inner_kernel(grid):
    def body(weights, factor, cot, e0, e1, e2, g0, g1, g2, u0, u1, u2, h1, l1, h2, l2, h3, l3, halves):
        ty, tx = places()
        store_matrix(matrix_3(weights), h3, l3)
        store_matrix(matrix_2(weights), h2, l2)
        store_matrix(matrix_1(weights), h1, l1)
        for r in range(2):
            g0[r] = roll(widen(e0[:, r, :]), BASE[0])
        for r, row in enumerate(factor_rows([widen(e1[:, r, :]) for r in range(4)], factor, 1, False)):
            g1[r] = row
        for r, row in enumerate(factor_rows([e2[:, r, :] for r in range(8)], factor, 2, False)):
            g2[r] = row
        for j in (0, 1):
            halves[j] = cot[:, :, 128 * j : 128 * (j + 1)].reshape(256, 128)
        left = beside(
            [
                stack([halves[j, pl.ds(2 * i + a, CH, stride=16), :] for i in range(8)])
                for a in (0, 1)
                for j in (0, 1)
            ]
        )
        out = mul3(split(left), (h3[...], l3[...]), NN)
        up2 = block_sum(out, 8, tile)
        side2 = block_sum(tile(out, 3), 8, lambda x, da: roll(x, -4 * da))
        top = inside_mask(HALO[2], tx, grid[1] - 1, False)
        ones = jnp.ones((1, 128), F32)
        up2 = clear_outside(up2, 1, ones, ty, grid[0] - 1)
        side2 = clear_outside(side2, 1, top, ty, grid[0] - 1)
        for r, row in enumerate(up2):
            u2[r] = row
        none = [jnp.zeros((CH, 128), F32)]
        up2, side2 = none + up2 + none, none + side2 + none
        left = beside(
            [stack(up2[0::2]), stack(up2[1::2]), stack(side2[0::2]) + roll(stack(side2[1::2]), 4)]
        )
        up1 = block_sum(mul3(split(left), (h2[...], l2[...]), NN), 6, tile)
        up1 = clear_outside(up1, 2, inside_mask(HALO[1], tx, grid[1] - 1, True), ty, grid[0] - 1)
        for r, row in enumerate(up1):
            u1[r] = row
        left = beside([stack(up1[0::2]), stack(up1[1::2])])
        up0 = block_sum(mul3(split(left), (h1[...], l1[...]), NN), 4, tile)
        for r, row in enumerate(up0):
            u0[r] = row

    return body


def second_kernel(grid):
    def body(got_a, got_b, g0, g1, g2, u0, u1, u2, send_a, send_b, x0, x1, s2, v0, v1, v2):
        ty, tx = places()
        lane = iota((CH, 128), 1)
        even = (tx & 1) == 0
        k = 0
        left, right, halo = [], [], []
        for j in (0, 1):
            first, second = got_a[j], got_b[j]
            right.append(jnp.where(even, first, second))
            left.append(jnp.where(even, second, first))
            halo.append(jnp.where((lane & 3) < 2, roll(left[j], -2), roll(right[j], 2)))

        def move(parts, k, offset, target, count):
            moved = roll(parts[k // 32], target - 4 * (k % 32) - offset)
            return jnp.where((lane >= target) & (lane < target + count), moved, 0.0)

        gs = []
        for level, ref in ((0, g0), (1, g1), (2, g2)):
            rows = []
            for r in range(ROWS[level]):
                side = move(halo, k, 0, HALO[level], 4)
                rows.append((ref[r], side) if level == 2 else ref[r] + side)
                k += 1
            gs.append(rows)
        us = []
        for level, ref in ((0, u0), (1, u1), (2, u2)):
            rows = []
            for r in range(ref.shape[0]):
                row = ref[r] + move(left, k, 2, BASE[level], 2)
                rows.append(row + move(right, k, 0, BASE[level] + COLS[level] - 2, 2))
                k += 1
            us.append(rows)

        inner0 = (lane >= BASE[0]) & (lane < BASE[0] + COLS[0])

        def payload(ends, ups):
            g = [[level[e] for e in ends] for level in gs]
            tiles = [row[0] for row in g[2]]
            tiles += [one + zero + two[1] for zero, one, two in zip(*g)]
            tiles.append(us[2][-ups])
            tiles += [
                jnp.where(inner0, us[0][e], us[1][e]) for e in ends
            ]
            return tiles

        low, high = payload((0, 1), 0), payload((-2, -1), 1)
        even = (ty & 1) == 0
        for j in range(len(low)):
            send_a[j] = jnp.where(even, high[j], low[j])
            send_b[j] = jnp.where(even, low[j], high[j])
        for ref, rows in ((x0, gs[0]), (x1, gs[1]), (s2, [row[1] for row in gs[2]])):
            for j, row in enumerate(rows):
                ref[j] = row
        for ref, rows, trim in ((v0, us[0], 2), (v1, us[1], 2), (v2, us[2], 1)):
            for j in range(ref.shape[0]):
                ref[j] = rows[j + trim]

    return body


def third_kernel(grid):
    def body(factor, got_a, got_b, x0, x1, g2, s2, v0, v1, v2, local, h1, l1, h2, l2, h3, l3, mix_h, mix_l, back0, back1, back2, sky, d0, d1, d2):
        ty, tx = places()
        even = (ty & 1) == 0
        above, below = [], []
        for j in range(7):
            first, second = got_a[j], got_b[j]
            above.append(jnp.where(even, second, first))
            below.append(jnp.where(even, first, second))

        def trio(rows):
            return beside([stack(rows[da : da + len(rows) - 2]) for da in (0, 1, 2)])

        field = above[2:4] + [x0[r] for r in range(2)] + below[2:4]
        out = mul3(split(trio(field)), (h1[...], l1[...]), NT)
        mixed = above[2:4] + [x1[r] for r in range(4)] + below[2:4]
        field = [tile(out[CH * i : CH * (i + 1)], a) for i in range(4) for a in (0, 1)]
        field = [f + m for f, m in zip(field, mixed)]
        mask = inside_mask(HALO[1], tx, grid[1] - 1, True)
        field = clear_outside(field, 2, mask, ty, grid[0] - 1)
        out = mul3(split(trio(field)), (h2[...], l2[...]), NT)
        mixed = above[0:2] + [g2[r] for r in range(8)] + below[0:2]
        side = above[2:4] + [s2[r] for r in range(8)] + below[2:4]
        pairs = [(out[CH * i : CH * (i + 1)], a) for i in range(6) for a in (0, 1)]
        field = [tile(o, a) + m for (o, a), m in zip(pairs, mixed)]
        side = [roll(tile(o, 2), -4 * a) + m for (o, a), m in zip(pairs, side)]
        field = clear_outside(field, 2, jnp.ones((1, 128), F32), ty, grid[0] - 1)[1:11]
        mask = inside_mask(HALO[2], tx, grid[1] - 1, False)
        side = clear_outside(side, 2, mask, ty, grid[0] - 1)[1:11]
        sides = [side[i] + roll(side[i + 1], 4) + roll(side[i + 2], 8) for i in range(8)]
        out = mul3(split(beside([trio(field), stack(sides)])), (h3[...], l3[...]), NT)
        fine = split(stack([out[:, :256], out[:, 256:]]))
        sky[...] = (mul3((mix_h[...], mix_l[...]), fine, NN) + local[...]).reshape(CH, 16, 256)

        up0 = [v0[r] + above[5 + r] + below[5 + r] for r in range(2)]
        up1 = [v1[0] + above[5], v1[1] + above[6], v1[2] + below[5], v1[3] + below[6]]
        up2 = [v2[0] + above[4]] + [v2[r] for r in range(1, 7)] + [v2[7] + below[4]]
        up1 = factor_rows(up1, factor, 1, True)
        up2 = factor_rows(up2, factor, 2, True)
        for ref, rows, back, level in ((d0, up0, back0, 0), (d1, up1, back1, 1), (d2, up2, back2, 2)):
            out = mul(back[...], stack(rows))
            cols = COLS[level]
            if BASE[level]:
                out = roll(out, -BASE[level])
            out = out.reshape(CH, ROWS[level], 128)
            ref[...] = out[:, :, :cols] if cols < 128 else out

    return body


def one_hot(test):
    return jnp.where(test, 1.0, 0.0)


def local_body(factor, mixing, cot, e3, local, grad, mix_h, mix_l, back0, back1, back2):
    f = mixing[...]
    column = one_hot(iota((256, CH), 0) // CH == iota((256, CH), 1))
    spread = mul(column, f)
    same = (iota((256, 256), 0) & 15) == (iota((256, 256), 1) & 15)

    def factored(ref, transposed):
        halves = [
            factor_tile(ref[:, :, 128 * h : 128 * (h + 1)].reshape(32, 8, 128), factor, transposed).reshape(256, 128)
            for h in (0, 1)
        ]
        return split(beside(halves))

    side = split(jnp.where(same, mul_t(column, spread), 0.0))
    grad[...] = mul3(side, factored(cot, True), NN).reshape(CH, 16, 256)
    side = split(jnp.where(same, mul_t(spread, column), 0.0))
    local[...] = mul3(side, factored(e3, False), NN)
    tiled = one_hot((iota((256, CH), 0) & 15) == iota((256, CH), 1))
    col = iota((256, 256), 1)
    there = (iota((256, 256), 0) & 15) == 2 * ((col & 127) >> 4) + (col >> 7)
    mix_h[...], mix_l[...] = split(jnp.where(there, mul_t(spread, tiled), 0.0))
    for ref, rows in ((back0, 2), (back1, 4), (back2, 8)):
        n = CH * rows
        full = mul_t(one_hot(iota((n, CH), 0) // rows == iota((n, CH), 1)), stack([f] * rows))
        ref[...] = jnp.where(iota((n, n), 0) % rows == iota((n, n), 1) // CH, full, 0.0)


def swaps(count, first):
    pairs = []
    for i in range(first, count - 1, 2):
        pairs += [(i, i + 1), (i + 1, i)]
    return pairs


def shaped(*shape, dtype=F32):
    return jax.ShapeDtypeStruct(shape, dtype)


SMEM = pl.BlockSpec(memory_space=pltpu.SMEM)
VMEM = pl.BlockSpec(memory_space=pltpu.VMEM)
HBM = pl.BlockSpec(memory_space=pltpu.HBM)


def call(body, specs, outs, args, scratch=(), limit=VMEM_LIMIT):
    return pl.pallas_call(
        body,
        out_shape=outs,
        in_specs=specs,
        out_specs=[VMEM] * len(outs),
        scratch_shapes=list(scratch),
        compiler_params=pltpu.CompilerParams(vmem_limit_bytes=limit),
    )(*args)


def device_body(grid):
    def on_device(e0, e1, e2, e3, weights, factor, mixing, cot):
        rows = [shaped(2, CH, 128), shaped(4, CH, 128), shaped(8, CH, 128)]
        ups = [shaped(6, CH, 128), shaped(8, CH, 128), shaped(10, CH, 128)]
        (send,) = call(
            first_kernel(grid),
            [HBM] * 6,
            [shaped(2, CH, 128)],
            (weights, factor, cot, e0, e1, e2),
            [
                pltpu.SMEM((3, 4, 9), F32),
                pltpu.SMEM((3, 4, 4), F32),
                pltpu.VMEM((CH, 16, 256), F32),
                pltpu.VMEM((CH, 2, 32), F32),
                pltpu.VMEM((CH, 4, 64), F32),
                pltpu.VMEM((CH, 8, 128), F32),
                pltpu.VMEM((256, 128), F32),
                pltpu.SemaphoreType.DMA((6,)),
            ],
            60 * 1024 * 1024,
        )
        got_a = lax.ppermute(send, "tx", swaps(grid[1], 0))
        got_b = lax.ppermute(send, "tx", swaps(grid[1], 1))
        sizes = [(256, 384), (384, 384), (512, 512)]
        inner = call(
            inner_kernel(grid),
            [SMEM] * 2 + [VMEM] * 4,
            rows + ups + [shaped(*size, dtype=BF16) for size in sizes for _ in (0, 1)],
            (weights, factor, cot, e0, e1, e2),
            [pltpu.VMEM((2, 256, 128), F32)],
        )
        matrices = inner[6:]
        second = call(
            second_kernel(grid),
            [VMEM] * 8,
            [shaped(7, CH, 128)] * 2 + rows + rows,
            (got_a, got_b, *inner[:6]),
        )
        local, grad3, *mixes = call(
            local_body,
            [SMEM] + [VMEM] * 3,
            [shaped(256, 256), shaped(CH, 16, 256)]
            + [shaped(256, 256, dtype=BF16)] * 2
            + [shaped(32, 32), shaped(64, 64), shaped(128, 128)],
            (factor, mixing, cot, e3),
        )
        got_a = lax.ppermute(second[0], "ty", swaps(grid[0], 0))
        got_b = lax.ppermute(second[1], "ty", swaps(grid[0], 1))
        x0, x1, s2, v0, v1, v2 = second[2:]
        sky, grad0, grad1, grad2 = call(
            third_kernel(grid),
            [SMEM] + [VMEM] * 21,
            [shaped(CH, 16, 256), shaped(CH, 2, 32), shaped(CH, 4, 64), shaped(CH, 8, 128)],
            (factor, got_a, got_b, x0, x1, inner[2], s2, v0, v1, v2, local, *matrices, *mixes),
        )
        return (sky, grad0, grad1, grad2, grad3)

    return on_device


def solution(mesh):
    tiles = P(None, "ty", "tx")
    return jax.shard_map(
        device_body((mesh.shape["ty"], mesh.shape["tx"])),
        mesh=mesh,
        in_specs=(tiles, tiles, tiles, tiles, P(), P(), P(), tiles),
        out_specs=(tiles,) * 5,
        check_vma=False,
    )
```

```python
import jax
import jax.numpy as jnp
from jax import lax
from jax.experimental import pallas as pl
from jax.experimental.pallas import tpu as pltpu
from jax.sharding import PartitionSpec as P

F32 = jnp.float32
BF16 = jnp.bfloat16
CH = 16
COLS = (32, 64, 128, 256)
ROWS = (2, 4, 8, 16)
BASE = (64, 0, 0, 0)
HALO = (96, 100, 104)
VMEM_LIMIT = 40 * 1024 * 1024


def iota(shape, dim):
    return lax.broadcasted_iota(jnp.int32, shape, dim)


def dot(left, right, dims, precision=None):
    return lax.dot_general(
        left, right, (dims, ((), ())), precision=precision, preferred_element_type=F32
    )


NN = ((1,), (0,))
NT = ((1,), (1,))


def mul(left, right):
    return dot(left, right, NN, lax.Precision.HIGHEST)


def mul_t(left, right):
    return dot(left, right, NT, lax.Precision.HIGHEST)


def split(x):
    high = x.astype(BF16)
    return high, (x - high.astype(F32)).astype(BF16)


def mul3(left, right, dims):
    return (
        dot(left[0], right[0], dims) + (dot(left[1], right[0], dims) + dot(left[0], right[1], dims))
    )


def roll(x, shift):
    shift %= 128
    return pltpu.roll(x, shift, 1) if shift else x


def places():
    return lax.axis_index("ty"), lax.axis_index("tx")


def refine_weight(weights, level, fine_col, coarse_col, a, da):
    step = coarse_col - (fine_col >> 1)
    odd = iota((1, 8, coarse_col.shape[2]), 1) & 1
    block = jnp.zeros(step.shape, F32)
    for db in (0, 1, 2):
        n = 3 * da + db
        pair = jnp.where(odd == 0, weights[level - 1, 2 * a, n], weights[level - 1, 2 * a + 1, n])
        block = jnp.where(step == db - 1, pair, block)
    return block.reshape(step.shape[0] * 8, step.shape[2])


def fine_index(count):
    shape = (count // 8, 8, 128)
    return iota(shape, 0) * 8 + iota(shape, 1)


def lane_index(count):
    return iota((count // 8, 8, 128), 2)


def interior_col(lane, level, none):
    cols, base = COLS[level], BASE[level]
    return jnp.where((lane >= base) & (lane < base + cols), lane - base, none)


def halo_col(lane, level, place, none):
    step = lane - place
    return jnp.where(
        (step >= 0) & (step < 4), jnp.where(step < 2, step - 2, step - 2 + COLS[level]), none
    )


def both_col(lane, level, none):
    return interior_col(lane, level, halo_col(lane, level, HALO[level], none))


FAR, NEAR = -4096, 4096


def zeros(count):
    return jnp.zeros((count, 128), F32)


def matrix_1(weights):
    group = iota((9, 8, 128), 0)
    fine = jnp.where(group < 8, group, HALO[1] // 8) * 8 + iota((9, 8, 128), 1)
    fine, coarse = both_col(fine, 1, FAR), both_col(lane_index(72), 0, NEAR)
    rows = []
    for a in (0, 1):
        row = []
        for da in (0, 1, 2):
            block = refine_weight(weights, 1, fine, coarse, a, da)
            row.append(stack([block[:64], zeros(32), block[64:], zeros(24)]))
        rows.append(row)
    return rows


def matrix_2(weights):
    index, coarse = fine_index(128), both_col(lane_index(128), 1, NEAR)
    rows = [[refine_weight(weights, 2, index, coarse, a, da) for da in (0, 1, 2)] for a in (0, 1)]
    index, coarse = HALO[2] + iota((1, 8, 128), 1), coarse[:1]
    halos = [halo_col(index, 2, HALO[2] + 4 * a, FAR) for a in (0, 1)]
    row = []
    for da in (0, 1, 2):
        block = sum(refine_weight(weights, 2, halos[a], coarse, a, da) for a in (0, 1))
        row.append(stack([zeros(HALO[2]), block, zeros(120 - HALO[2])]))
    rows.append(row)
    return rows


def matrix_3(weights):
    index, lane = fine_index(256), lane_index(256)
    ends = iota((2, 8, 128), 0) * 248 + iota((2, 8, 128), 1)
    halos = [halo_col(lane_index(16), 2, HALO[2] + 4 * da, NEAR) for da in (0, 1, 2)]
    rows = []
    for a in (0, 1):
        row = [refine_weight(weights, 3, index, lane, a, da) for da in (0, 1, 2)]
        block = sum(refine_weight(weights, 3, ends, halos[da], a, da) for da in (0, 1, 2))
        row.append(stack([block[:8], zeros(240), block[8:]]))
        rows.append(row)
    return rows


def store_matrix(blocks, high_ref, low_ref):
    down = 0
    for row in blocks:
        for j, block in enumerate(row):
            high, low = split(block)
            high_ref[down : down + block.shape[0], 128 * j : 128 * (j + 1)] = high
            low_ref[down : down + block.shape[0], 128 * j : 128 * (j + 1)] = low
        down += row[0].shape[0]


def stack(rows):
    return jnp.concatenate(rows, axis=0)


def beside(parts):
    return jnp.concatenate(parts, axis=1)


def block_sum(out, blocks, part):
    result = []
    for i in range(-1, blocks + 1):
        total = None
        for da in (0, 1, 2):
            block = i - (da - 1)
            if 0 <= block < blocks:
                term = part(out[CH * block : CH * (block + 1)], da)
                total = term if total is None else total + term
        result.append(total)
    return result


def tile(x, j):
    return x[:, 128 * j : 128 * (j + 1)]


def swap_lanes(x):
    axis = x.ndim - 1
    lane = iota(x.shape, axis)
    return jnp.where((lane & 1) == 0, pltpu.roll(x, x.shape[axis] - 1, axis), pltpu.roll(x, 1, axis))


def factor_rows(rows, factor, level, transposed):
    odd = iota(rows[0].shape, 1) & 1
    swapped = [swap_lanes(r) for r in rows]

    def entry(a, b, a2, b2):
        if transposed:
            return factor[level - 1, 2 * a2 + b2, 2 * a + b]
        return factor[level - 1, 2 * a + b, 2 * a2 + b2]

    pairs = {}
    for a in (0, 1):
        for a2 in (0, 1):
            pairs[a, a2] = (
                jnp.where(odd == 0, entry(a, 0, a2, 0), entry(a, 1, a2, 1)),
                jnp.where(odd == 0, entry(a, 0, a2, 1), entry(a, 1, a2, 0)),
            )
    result = []
    for i in range(len(rows) // 2):
        for a in (0, 1):
            total = None
            for a2 in (0, 1):
                same, other = pairs[a, a2]
                term = same * rows[2 * i + a2] + other * swapped[2 * i + a2]
                total = term if total is None else total + term
            result.append(total)
    return result


def factor_tile(x, factor, transposed):
    odd_row = iota((1, 8, 128), 1) & 1
    odd_col = iota((1, 8, 128), 2) & 1
    side = swap_lanes(x)

    def swap_rows(y):
        row = iota(y.shape, 1)
        return jnp.where((row & 1) == 0, pltpu.roll(y, 7, 1), pltpu.roll(y, 1, 1))

    def coefficient(flip_row, flip_col):
        values = []
        for a in (0, 1):
            for b in (0, 1):
                here, there = 2 * a + b, 2 * (a ^ flip_row) + (b ^ flip_col)
                values.append(factor[2, there, here] if transposed else factor[2, here, there])
        return jnp.where(
            odd_row == 0,
            jnp.where(odd_col == 0, values[0], values[1]),
            jnp.where(odd_col == 0, values[2], values[3]),
        )

    return (
        coefficient(0, 0) * x
        + coefficient(0, 1) * side
        + coefficient(1, 0) * swap_rows(x)
        + coefficient(1, 1) * swap_rows(side)
    )


def inside_mask(place, tx, last, keep_rest):
    lane = iota((1, 128), 1) - place
    left = jnp.where(tx == 0, 0.0, 1.0)
    right = jnp.where(tx == last, 0.0, 1.0)
    rest = jnp.full((1, 128), 1.0 if keep_rest else 0.0, F32)
    return jnp.where((lane >= 0) & (lane < 2), left, jnp.where((lane >= 2) & (lane < 4), right, rest))


def clear_outside(rows, around, mask, ty, last):
    top = jnp.where(ty == 0, 0.0, 1.0)
    bottom = jnp.where(ty == last, 0.0, 1.0)
    result = []
    for k, row in enumerate(rows):
        if k < around:
            row = row * (mask * top)
        elif k >= len(rows) - around:
            row = row * (mask * bottom)
        else:
            row = row * mask
        result.append(row)
    return result


def edge_col(lane, level, none):
    inside = (0, 2, 6, 16)[level]
    cols = COLS[level]
    if level == 3:
        return jnp.where(lane < 16, lane, jnp.where(lane < 32, cols + lane - 32, none))
    col = jnp.where(lane < 2, lane - 2, jnp.where(lane < 4, cols + lane - 2, none))
    col = jnp.where((lane >= 4) & (lane < 4 + inside), lane - 4, col)
    return jnp.where(
        (lane >= 4 + inside) & (lane < 4 + 2 * inside), cols - inside + lane - 4 - inside, col
    )


def edge_matrix(weights, level, width):
    fine = edge_col(fine_index(width), level, FAR)
    coarse = edge_col(lane_index(width), level - 1, NEAR)
    return split(
        stack([beside([refine_weight(weights, level, fine, coarse, a, da) for da in (0, 1, 2)]) for a in (0, 1)])
    )


def edge_pull(rows, matrix, width):
    even, odd = stack(rows[0::2]), stack(rows[1::2])
    left = jnp.where(iota(even.shape, 1) < width, even, roll(odd, width))[:, : 2 * width]
    return block_sum(mul3(split(left), matrix, NN), len(rows) // 2, tile)


def widen(x):
    if x.shape[1] == 128:
        return x
    return beside([x, jnp.zeros((x.shape[0], 128 - x.shape[1]), F32)])


def first_kernel(grid):
    def body(weights_in, factor_in, cot_in, e0_in, e1_in, e2_in, send, weights, factor, cot, e0, e1, e2, edge, sems):
        copies = [
            pltpu.make_async_copy(source, target, sems.at[k])
            for k, (source, target) in enumerate(
                ((cot_in, cot), (weights_in, weights), (factor_in, factor), (e0_in, e0), (e1_in, e1), (e2_in, e2))
            )
        ]
        for copy in copies:
            copy.start()
        ty, tx = places()
        lane = iota((CH, 128), 1)
        for copy in copies[1:]:
            copy.wait()
        edges = [edge_matrix(weights, level, (0, 8, 16, 32)[level]) for level in (1, 2, 3)]

        def ends(row, level):
            return jnp.where(lane < 2, row, roll(row, 4 - COLS[level]))

        pieces = [ends(widen(e0[:, r, :]), 0) for r in range(2)]
        pieces += factor_rows([ends(widen(e1[:, r, :]), 1) for r in range(4)], factor, 1, False)
        pieces += factor_rows([ends(e2[:, r, :], 2) for r in range(8)], factor, 2, False)
        copies[0].wait()
        low = cot[:, :, :128].reshape(256, 128)
        high = cot[:, :, 128:].reshape(256, 128)
        edge[...] = jnp.where(iota((256, 128), 1) < 16, low, roll(high, 32))
        rows = [edge[pl.ds(r, CH, stride=16), :] for r in range(16)]
        mask = inside_mask(0, tx, grid[1] - 1, True)
        up2 = clear_outside(edge_pull(rows, edges[2], 32), 1, mask, ty, grid[0] - 1)
        none = jnp.zeros((CH, 128), F32)
        up1 = edge_pull([none] + up2 + [none], edges[1], 16)
        up1 = clear_outside(up1, 2, mask, ty, grid[0] - 1)
        up0 = edge_pull(up1, edges[0], 8)
        pieces += up0 + up1 + up2
        totals = [none, none]
        for k, piece in enumerate(pieces):
            at = 4 * (k % 32)
            totals[k // 32] = jnp.where((lane >= at) & (lane < at + 4), roll(piece, at), totals[k // 32])
        send[0] = totals[0]
        send[1] = totals[1]

    return body


def inner_kernel(grid):
    def body(weights, factor, cot, e0, e1, e2, g0, g1, g2, u0, u1, u2, h1, l1, h2, l2, h3, l3, halves):
        ty, tx = places()
        store_matrix(matrix_3(weights), h3, l3)
        store_matrix(matrix_2(weights), h2, l2)
        store_matrix(matrix_1(weights), h1, l1)
        for r in range(2):
            g0[r] = roll(widen(e0[:, r, :]), BASE[0])
        for r, row in enumerate(factor_rows([widen(e1[:, r, :]) for r in range(4)], factor, 1, False)):
            g1[r] = row
        for r, row in enumerate(factor_rows([e2[:, r, :] for r in range(8)], factor, 2, False)):
            g2[r] = row
        for j in (0, 1):
            halves[j] = cot[:, :, 128 * j : 128 * (j + 1)].reshape(256, 128)
        left = beside(
            [
                stack([halves[j, pl.ds(2 * i + a, CH, stride=16), :] for i in range(8)])
                for a in (0, 1)
                for j in (0, 1)
            ]
        )
        out = mul3(split(left), (h3[...], l3[...]), NN)
        up2 = block_sum(out, 8, tile)
        side2 = block_sum(tile(out, 3), 8, lambda x, da: roll(x, -4 * da))
        top = inside_mask(HALO[2], tx, grid[1] - 1, False)
        ones = jnp.ones((1, 128), F32)
        up2 = clear_outside(up2, 1, ones, ty, grid[0] - 1)
        side2 = clear_outside(side2, 1, top, ty, grid[0] - 1)
        for r, row in enumerate(up2):
            u2[r] = row
        none = [jnp.zeros((CH, 128), F32)]
        up2, side2 = none + up2 + none, none + side2 + none
        left = beside(
            [stack(up2[0::2]), stack(up2[1::2]), stack(side2[0::2]) + roll(stack(side2[1::2]), 4)]
        )
        up1 = block_sum(mul3(split(left), (h2[...], l2[...]), NN), 6, tile)
        up1 = clear_outside(up1, 2, inside_mask(HALO[1], tx, grid[1] - 1, True), ty, grid[0] - 1)
        for r, row in enumerate(up1):
            u1[r] = row
        left = beside([stack(up1[0::2]), stack(up1[1::2])])
        up0 = block_sum(mul3(split(left), (h1[...], l1[...]), NN), 4, tile)
        for r, row in enumerate(up0):
            u0[r] = row

    return body


def second_kernel(grid):
    def body(got_a, got_b, g0, g1, g2, u0, u1, u2, send_a, send_b, x0, x1, s2, v0, v1, v2):
        ty, tx = places()
        lane = iota((CH, 128), 1)
        even = (tx & 1) == 0
        k = 0
        left, right, halo = [], [], []
        for j in (0, 1):
            first, second = got_a[j], got_b[j]
            right.append(jnp.where(even, first, second))
            left.append(jnp.where(even, second, first))
            halo.append(jnp.where((lane & 3) < 2, roll(left[j], -2), roll(right[j], 2)))

        def move(parts, k, offset, target, count):
            moved = roll(parts[k // 32], target - 4 * (k % 32) - offset)
            return jnp.where((lane >= target) & (lane < target + count), moved, 0.0)

        gs = []
        for level, ref in ((0, g0), (1, g1), (2, g2)):
            rows = []
            for r in range(ROWS[level]):
                side = move(halo, k, 0, HALO[level], 4)
                rows.append((ref[r], side) if level == 2 else ref[r] + side)
                k += 1
            gs.append(rows)
        us = []
        for level, ref in ((0, u0), (1, u1), (2, u2)):
            rows = []
            for r in range(ref.shape[0]):
                row = ref[r] + move(left, k, 2, BASE[level], 2)
                rows.append(row + move(right, k, 0, BASE[level] + COLS[level] - 2, 2))
                k += 1
            us.append(rows)

        inner0 = (lane >= BASE[0]) & (lane < BASE[0] + COLS[0])

        def payload(ends, ups):
            g = [[level[e] for e in ends] for level in gs]
            tiles = [row[0] for row in g[2]]
            tiles += [one + zero + two[1] for zero, one, two in zip(*g)]
            tiles.append(us[2][-ups])
            tiles += [
                jnp.where(inner0, us[0][e], us[1][e]) for e in ends
            ]
            return tiles

        low, high = payload((0, 1), 0), payload((-2, -1), 1)
        even = (ty & 1) == 0
        for j in range(len(low)):
            send_a[j] = jnp.where(even, high[j], low[j])
            send_b[j] = jnp.where(even, low[j], high[j])
        for ref, rows in ((x0, gs[0]), (x1, gs[1]), (s2, [row[1] for row in gs[2]])):
            for j, row in enumerate(rows):
                ref[j] = row
        for ref, rows, trim in ((v0, us[0], 2), (v1, us[1], 2), (v2, us[2], 1)):
            for j in range(ref.shape[0]):
                ref[j] = rows[j + trim]

    return body


def third_kernel(grid):
    def body(factor, got_a, got_b, x0, x1, g2, s2, v0, v1, v2, local, h1, l1, h2, l2, h3, l3, mix_h, mix_l, back0, back1, back2, sky, d0, d1, d2):
        ty, tx = places()
        even = (ty & 1) == 0
        above, below = [], []
        for j in range(7):
            first, second = got_a[j], got_b[j]
            above.append(jnp.where(even, second, first))
            below.append(jnp.where(even, first, second))

        def trio(rows):
            return beside([stack(rows[da : da + len(rows) - 2]) for da in (0, 1, 2)])

        field = above[2:4] + [x0[r] for r in range(2)] + below[2:4]
        out = mul3(split(trio(field)), (h1[...], l1[...]), NT)
        mixed = above[2:4] + [x1[r] for r in range(4)] + below[2:4]
        field = [tile(out[CH * i : CH * (i + 1)], a) for i in range(4) for a in (0, 1)]
        field = [f + m for f, m in zip(field, mixed)]
        mask = inside_mask(HALO[1], tx, grid[1] - 1, True)
        field = clear_outside(field, 2, mask, ty, grid[0] - 1)
        out = mul3(split(trio(field)), (h2[...], l2[...]), NT)
        mixed = above[0:2] + [g2[r] for r in range(8)] + below[0:2]
        side = above[2:4] + [s2[r] for r in range(8)] + below[2:4]
        pairs = [(out[CH * i : CH * (i + 1)], a) for i in range(6) for a in (0, 1)]
        field = [tile(o, a) + m for (o, a), m in zip(pairs, mixed)]
        side = [roll(tile(o, 2), -4 * a) + m for (o, a), m in zip(pairs, side)]
        field = clear_outside(field, 2, jnp.ones((1, 128), F32), ty, grid[0] - 1)[1:11]
        mask = inside_mask(HALO[2], tx, grid[1] - 1, False)
        side = clear_outside(side, 2, mask, ty, grid[0] - 1)[1:11]
        sides = [side[i] + roll(side[i + 1], 4) + roll(side[i + 2], 8) for i in range(8)]
        out = mul3(split(beside([trio(field), stack(sides)])), (h3[...], l3[...]), NT)
        fine = split(stack([out[:, :256], out[:, 256:]]))
        sky[...] = (mul3((mix_h[...], mix_l[...]), fine, NN) + local[...]).reshape(CH, 16, 256)

        up0 = [v0[r] + above[5 + r] + below[5 + r] for r in range(2)]
        up1 = [v1[0] + above[5], v1[1] + above[6], v1[2] + below[5], v1[3] + below[6]]
        up2 = [v2[0] + above[4]] + [v2[r] for r in range(1, 7)] + [v2[7] + below[4]]
        up1 = factor_rows(up1, factor, 1, True)
        up2 = factor_rows(up2, factor, 2, True)
        for ref, rows, back, level in ((d0, up0, back0, 0), (d1, up1, back1, 1), (d2, up2, back2, 2)):
            out = mul(back[...], stack(rows))
            cols = COLS[level]
            if BASE[level]:
                out = roll(out, -BASE[level])
            out = out.reshape(CH, ROWS[level], 128)
            ref[...] = out[:, :, :cols] if cols < 128 else out

    return body


def one_hot(test):
    return jnp.where(test, 1.0, 0.0).astype(BF16)


def local_body(factor, mixing, cot, e3, local, grad_out, mix_h, mix_l, back0, back1, back2, grad, sem):
    parts = split(mixing[...])
    column = one_hot(iota((256, CH), 0) // CH == iota((256, CH), 1))
    spread = [dot(column, f, NN).astype(BF16) for f in parts]
    same = (iota((256, 256), 0) & 15) == (iota((256, 256), 1) & 15)

    def select(where, pairs):
        return [jnp.where(where, dot(x, y, NT), 0.0).astype(BF16) for x, y in pairs]

    def factored(ref, transposed):
        halves = [
            factor_tile(ref[:, :, 128 * h : 128 * (h + 1)].reshape(32, 8, 128), factor, transposed).reshape(256, 128)
            for h in (0, 1)
        ]
        return split(beside(halves))

    side = select(same, [(column, f) for f in spread])
    grad[...] = mul3(side, factored(cot, True), NN).reshape(CH, 16, 256)
    copy = pltpu.make_async_copy(grad, grad_out, sem)
    copy.start()
    side = select(same, [(f, column) for f in spread])
    local[...] = mul3(side, factored(e3, False), NN)
    tiled = one_hot((iota((256, CH), 0) & 15) == iota((256, CH), 1))
    col = iota((256, 256), 1)
    there = (iota((256, 256), 0) & 15) == 2 * ((col & 127) >> 4) + (col >> 7)
    mix_h[...], mix_l[...] = select(there, [(f, tiled) for f in spread])
    for ref, rows in ((back0, 2), (back1, 4), (back2, 8)):
        n = CH * rows
        one = one_hot(iota((n, CH), 0) // rows == iota((n, CH), 1))
        full = [dot(one, stack([f] * rows), NT) for f in parts]
        ref[...] = jnp.where(iota((n, n), 0) % rows == iota((n, n), 1) // CH, full[0] + full[1], 0.0)
    copy.wait()


def swaps(count, first):
    pairs = []
    for i in range(first, count - 1, 2):
        pairs += [(i, i + 1), (i + 1, i)]
    return pairs


def shaped(*shape, dtype=F32):
    return jax.ShapeDtypeStruct(shape, dtype)


SMEM = pl.BlockSpec(memory_space=pltpu.SMEM)
VMEM = pl.BlockSpec(memory_space=pltpu.VMEM)
HBM = pl.BlockSpec(memory_space=pltpu.HBM)


def call(body, specs, outs, args, scratch=(), limit=VMEM_LIMIT, into=None):
    return pl.pallas_call(
        body,
        out_shape=outs,
        in_specs=specs,
        out_specs=[HBM if k == into else VMEM for k in range(len(outs))],
        scratch_shapes=list(scratch),
        compiler_params=pltpu.CompilerParams(vmem_limit_bytes=limit),
    )(*args)


def device_body(grid):
    def on_device(e0, e1, e2, e3, weights, factor, mixing, cot):
        rows = [shaped(2, CH, 128), shaped(4, CH, 128), shaped(8, CH, 128)]
        ups = [shaped(6, CH, 128), shaped(8, CH, 128), shaped(10, CH, 128)]
        (send,) = call(
            first_kernel(grid),
            [HBM] * 6,
            [shaped(2, CH, 128)],
            (weights, factor, cot, e0, e1, e2),
            [
                pltpu.SMEM((3, 4, 9), F32),
                pltpu.SMEM((3, 4, 4), F32),
                pltpu.VMEM((CH, 16, 256), F32),
                pltpu.VMEM((CH, 2, 32), F32),
                pltpu.VMEM((CH, 4, 64), F32),
                pltpu.VMEM((CH, 8, 128), F32),
                pltpu.VMEM((256, 128), F32),
                pltpu.SemaphoreType.DMA((6,)),
            ],
            60 * 1024 * 1024,
        )
        got_a = lax.ppermute(send, "tx", swaps(grid[1], 0))
        got_b = lax.ppermute(send, "tx", swaps(grid[1], 1))
        sizes = [(256, 384), (384, 384), (512, 512)]
        inner = call(
            inner_kernel(grid),
            [SMEM] * 2 + [VMEM] * 4,
            rows + ups + [shaped(*size, dtype=BF16) for size in sizes for _ in (0, 1)],
            (weights, factor, cot, e0, e1, e2),
            [pltpu.VMEM((2, 256, 128), F32)],
        )
        matrices = inner[6:]
        second = call(
            second_kernel(grid),
            [VMEM] * 8,
            [shaped(7, CH, 128)] * 2 + rows + rows,
            (got_a, got_b, *inner[:6]),
        )
        local, grad3, *mixes = call(
            local_body,
            [SMEM] + [VMEM] * 3,
            [shaped(256, 256), shaped(CH, 16, 256)]
            + [shaped(256, 256, dtype=BF16)] * 2
            + [shaped(32, 32), shaped(64, 64), shaped(128, 128)],
            (factor, mixing, cot, e3),
            [pltpu.VMEM((CH, 16, 256), F32), pltpu.SemaphoreType.DMA],
            into=1,
        )
        got_a = lax.ppermute(second[0], "ty", swaps(grid[0], 0))
        got_b = lax.ppermute(second[1], "ty", swaps(grid[0], 1))
        x0, x1, s2, v0, v1, v2 = second[2:]
        sky, grad0, grad1, grad2 = call(
            third_kernel(grid),
            [SMEM] + [VMEM] * 21,
            [shaped(CH, 16, 256), shaped(CH, 2, 32), shaped(CH, 4, 64), shaped(CH, 8, 128)],
            (factor, got_a, got_b, x0, x1, inner[2], s2, v0, v1, v2, local, *matrices, *mixes),
        )
        return (sky, grad0, grad1, grad2, grad3)

    return on_device


def solution(mesh):
    tiles = P(None, "ty", "tx")
    return jax.shard_map(
        device_body((mesh.shape["ty"], mesh.shape["tx"])),
        mesh=mesh,
        in_specs=(tiles, tiles, tiles, tiles, P(), P(), P(), tiles),
        out_specs=(tiles,) * 5,
        check_vma=False,
    )
```

```python
import jax
import jax.numpy as jnp
from jax import lax
from jax.experimental import pallas as pl
from jax.experimental.pallas import tpu as pltpu
from jax.sharding import PartitionSpec as P

F32 = jnp.float32
BF16 = jnp.bfloat16
CH = 16
COLS = (32, 64, 128, 256)
ROWS = (2, 4, 8, 16)
BASE = (64, 0, 0, 0)
HALO = (96, 100, 104)
VMEM_LIMIT = 40 * 1024 * 1024


def iota(shape, dim):
    return lax.broadcasted_iota(jnp.int32, shape, dim)


def dot(left, right, dims, precision=None):
    return lax.dot_general(
        left, right, (dims, ((), ())), precision=precision, preferred_element_type=F32
    )


NN = ((1,), (0,))
NT = ((1,), (1,))


def mul(left, right):
    return dot(left, right, NN, lax.Precision.HIGHEST)


def mul_t(left, right):
    return dot(left, right, NT, lax.Precision.HIGHEST)


def split(x):
    high = x.astype(BF16)
    return high, (x - high.astype(F32)).astype(BF16)


def mul3(left, right, dims):
    return (
        dot(left[0], right[0], dims) + (dot(left[1], right[0], dims) + dot(left[0], right[1], dims))
    )


def roll(x, shift):
    shift %= 128
    return pltpu.roll(x, shift, 1) if shift else x


def places():
    return lax.axis_index("ty"), lax.axis_index("tx")


def refine_weight(weights, level, fine_col, coarse_col, a, da, along):
    step = coarse_col - (fine_col >> 1)
    odd = iota((1, 8, step.shape[2]), along) & 1
    block = jnp.zeros(step.shape, F32)
    for db in (0, 1, 2):
        n = 3 * da + db
        pair = jnp.where(odd == 0, weights[level - 1, 2 * a, n], weights[level - 1, 2 * a + 1, n])
        block = jnp.where(step == db - 1, pair, block)
    return block.reshape(step.shape[0] * 8, step.shape[2])


def fine_index(count):
    shape = (count // 8, 8, 128)
    return iota(shape, 0) * 8 + iota(shape, 1)


def lane_index(count):
    return iota((count // 8, 8, 128), 2)


def interior_col(lane, level, none):
    cols, base = COLS[level], BASE[level]
    return jnp.where((lane >= base) & (lane < base + cols), lane - base, none)


def halo_col(lane, level, place, none):
    step = lane - place
    return jnp.where(
        (step >= 0) & (step < 4), jnp.where(step < 2, step - 2, step - 2 + COLS[level]), none
    )


def both_col(lane, level, none):
    return interior_col(lane, level, halo_col(lane, level, HALO[level], none))


FAR, NEAR = -4096, 4096


def zeros(count):
    return jnp.zeros((count, 128), F32)


def lane_range(start, count):
    return iota((1, 8, count), 2) + start


def sublane_range(start, groups):
    return iota((groups, 8, 128), 0) * 8 + iota((groups, 8, 128), 1) + start


def matrix_1(weights):
    coarse, fine = both_col(sublane_range(BASE[0], 5), 0, NEAR), both_col(lane_range(0, 128), 1, FAR)
    rows = []
    for da in (0, 1, 2):
        row = []
        for a in (0, 1):
            block = refine_weight(weights, 1, fine, coarse, a, da, 2)
            row.append(stack([zeros(BASE[0]), block, zeros(88 - BASE[0])]))
        rows.append(row)
    return rows


def matrix_2(weights):
    group = iota((9, 8, 128), 0)
    coarse = jnp.where(group < 8, group, HALO[1] // 8) * 8 + iota((9, 8, 128), 1)
    coarse, lane = both_col(coarse, 1, NEAR), lane_range(0, 128)
    halos = [halo_col(lane, 2, HALO[2] + 4 * a, FAR) for a in (0, 1)]
    rows = []
    for da in (0, 1, 2):
        row = [refine_weight(weights, 2, lane, coarse, a, da, 2) for a in (0, 1)]
        row.append(sum(refine_weight(weights, 2, halos[a], coarse, a, da, 2) for a in (0, 1)))
        rows.append([stack([x[:64], zeros(32), x[64:], zeros(24)]) for x in row])
    return rows


def matrix_3(weights):
    index = sublane_range(0, 16)
    halo = sublane_range(HALO[2], 2)
    rows = []
    for da in (0, 1, 2):
        rows.append(
            [refine_weight(weights, 3, lane_range(128 * h, 128), index, a, da, 2) for a in (0, 1) for h in (0, 1)]
        )
    row = []
    for a in (0, 1):
        for h in (0, 1):
            block = sum(
                refine_weight(
                    weights, 3, lane_range(128 * h, 128), halo_col(halo, 2, HALO[2] + 4 * da, NEAR), a, da, 2
                )
                for da in (0, 1, 2)
            )
            row.append(stack([zeros(HALO[2]), block, zeros(112 - HALO[2])]))
    rows.append(row)
    return rows


def store_matrix(blocks, high_ref, low_ref):
    down = 0
    for row in blocks:
        for j, block in enumerate(row):
            high, low = split(block)
            high_ref[down : down + block.shape[0], 128 * j : 128 * (j + 1)] = high
            low_ref[down : down + block.shape[0], 128 * j : 128 * (j + 1)] = low
        down += row[0].shape[0]


def stack(rows):
    return jnp.concatenate(rows, axis=0)


def beside(parts):
    return jnp.concatenate(parts, axis=1)


def block_sum(out, blocks, part):
    result = []
    for i in range(-1, blocks + 1):
        total = None
        for da in (0, 1, 2):
            block = i - (da - 1)
            if 0 <= block < blocks:
                term = part(out[CH * block : CH * (block + 1)], da)
                total = term if total is None else total + term
        result.append(total)
    return result


def tile(x, j):
    return x[:, 128 * j : 128 * (j + 1)]


def swap_lanes(x):
    axis = x.ndim - 1
    lane = iota(x.shape, axis)
    return jnp.where((lane & 1) == 0, pltpu.roll(x, x.shape[axis] - 1, axis), pltpu.roll(x, 1, axis))


def factor_rows(rows, factor, level, transposed):
    odd = iota(rows[0].shape, 1) & 1
    swapped = [swap_lanes(r) for r in rows]

    def entry(a, b, a2, b2):
        if transposed:
            return factor[level - 1, 2 * a2 + b2, 2 * a + b]
        return factor[level - 1, 2 * a + b, 2 * a2 + b2]

    pairs = {}
    for a in (0, 1):
        for a2 in (0, 1):
            pairs[a, a2] = (
                jnp.where(odd == 0, entry(a, 0, a2, 0), entry(a, 1, a2, 1)),
                jnp.where(odd == 0, entry(a, 0, a2, 1), entry(a, 1, a2, 0)),
            )
    result = []
    for i in range(len(rows) // 2):
        for a in (0, 1):
            total = None
            for a2 in (0, 1):
                same, other = pairs[a, a2]
                term = same * rows[2 * i + a2] + other * swapped[2 * i + a2]
                total = term if total is None else total + term
            result.append(total)
    return result


def factor_tile(x, factor, transposed):
    odd_row = iota((1, 8, 128), 1) & 1
    odd_col = iota((1, 8, 128), 2) & 1
    side = swap_lanes(x)

    def swap_rows(y):
        row = iota(y.shape, 1)
        return jnp.where((row & 1) == 0, pltpu.roll(y, 7, 1), pltpu.roll(y, 1, 1))

    def coefficient(flip_row, flip_col):
        values = []
        for a in (0, 1):
            for b in (0, 1):
                here, there = 2 * (a ^ flip_row) + b, 2 * a + (b ^ flip_col)
                values.append(factor[2, there, here] if transposed else factor[2, here, there])
        return jnp.where(
            odd_row == 0,
            jnp.where(odd_col == 0, values[0], values[1]),
            jnp.where(odd_col == 0, values[2], values[3]),
        )

    return (
        coefficient(0, 0) * x
        + coefficient(0, 1) * side
        + swap_rows(coefficient(1, 0) * x + coefficient(1, 1) * side)
    )


def inside_mask(place, tx, last, keep_rest):
    lane = iota((1, 128), 1) - place
    left = jnp.where(tx == 0, 0.0, 1.0)
    right = jnp.where(tx == last, 0.0, 1.0)
    rest = jnp.full((1, 128), 1.0 if keep_rest else 0.0, F32)
    return jnp.where((lane >= 0) & (lane < 2), left, jnp.where((lane >= 2) & (lane < 4), right, rest))


def clear_outside(rows, around, mask, ty, last):
    top = jnp.where(ty == 0, 0.0, 1.0)
    bottom = jnp.where(ty == last, 0.0, 1.0)
    result = []
    for k, row in enumerate(rows):
        if k < around:
            row = row * (mask * top)
        elif k >= len(rows) - around:
            row = row * (mask * bottom)
        else:
            row = row * mask
        result.append(row)
    return result


def edge_col(lane, level, none):
    inside = (0, 2, 6, 16)[level]
    cols = COLS[level]
    if level == 3:
        return jnp.where(lane < 16, lane, jnp.where(lane < 32, cols + lane - 32, none))
    col = jnp.where(lane < 2, lane - 2, jnp.where(lane < 4, cols + lane - 2, none))
    col = jnp.where((lane >= 4) & (lane < 4 + inside), lane - 4, col)
    return jnp.where(
        (lane >= 4 + inside) & (lane < 4 + 2 * inside), cols - inside + lane - 4 - inside, col
    )


def edge_matrix(weights, level, width):
    fine = edge_col(fine_index(width), level, FAR)
    coarse = edge_col(lane_index(width), level - 1, NEAR)
    return split(
        stack([beside([refine_weight(weights, level, fine, coarse, a, da, 1) for da in (0, 1, 2)]) for a in (0, 1)])
    )


def edge_pull(rows, matrix, width):
    even, odd = stack(rows[0::2]), stack(rows[1::2])
    left = jnp.where(iota(even.shape, 1) < width, even, roll(odd, width))[:, : 2 * width]
    return block_sum(mul3(split(left), matrix, NN), len(rows) // 2, tile)


def widen(x):
    if x.shape[1] == 128:
        return x
    return beside([x, jnp.zeros((x.shape[0], 128 - x.shape[1]), F32)])


def first_kernel(grid):
    def body(weights_in, factor_in, cot_in, e0_in, e1_in, e2_in, send, weights, factor, cot, e0, e1, e2, edge, sems):
        copies = [
            pltpu.make_async_copy(source, target, sems.at[k])
            for k, (source, target) in enumerate(
                ((weights_in, weights), (factor_in, factor), (e0_in, e0), (e1_in, e1), (e2_in, e2))
            )
        ]
        for q in range(4):
            part = pl.ds(4 * q, 4)
            copies.append(pltpu.make_async_copy(cot_in.at[part], cot.at[part], sems.at[5 + q]))
        for copy in copies:
            copy.start()
        ty, tx = places()
        lane = iota((CH, 128), 1)
        for copy in copies[:5]:
            copy.wait()
        edges = [edge_matrix(weights, level, (0, 8, 16, 32)[level]) for level in (1, 2, 3)]

        def ends(row, level):
            return jnp.where(lane < 2, row, roll(row, 4 - COLS[level]))

        pieces = [ends(widen(e0[:, r, :]), 0) for r in range(2)]
        pieces += factor_rows([ends(widen(e1[:, r, :]), 1) for r in range(4)], factor, 1, False)
        pieces += factor_rows([ends(e2[:, r, :], 2) for r in range(8)], factor, 2, False)
        for copy in copies[5:]:
            copy.wait()
        low = cot[:, :, :128].reshape(256, 128)
        high = cot[:, :, 128:].reshape(256, 128)
        edge[...] = jnp.where(iota((256, 128), 1) < 16, low, roll(high, 32))
        rows = [edge[pl.ds(r, CH, stride=16), :] for r in range(16)]
        mask = inside_mask(0, tx, grid[1] - 1, True)
        up2 = clear_outside(edge_pull(rows, edges[2], 32), 1, mask, ty, grid[0] - 1)
        none = jnp.zeros((CH, 128), F32)
        up1 = edge_pull([none] + up2 + [none], edges[1], 16)
        up1 = clear_outside(up1, 2, mask, ty, grid[0] - 1)
        up0 = edge_pull(up1, edges[0], 8)
        pieces += up0 + up1 + up2
        totals = [none, none]
        for k, piece in enumerate(pieces):
            at = 4 * (k % 32)
            totals[k // 32] = jnp.where((lane >= at) & (lane < at + 4), roll(piece, at), totals[k // 32])
        send[0] = totals[0]
        send[1] = totals[1]

    return body


def one_hot(test):
    return jnp.where(test, 1.0, 0.0).astype(BF16)


def spread_factor(mixing):
    parts = split(mixing[...])
    column = one_hot(iota((256, CH), 0) // CH == iota((256, CH), 1))
    return parts, column, [dot(column, f, NN).astype(BF16) for f in parts]


def select(where, pairs):
    return [jnp.where(where, dot(x, y, NT), 0.0).astype(BF16) for x, y in pairs]


def side_matrices(mixing, side_h, side_l, back_h, back_l):
    _, column, spread = spread_factor(mixing)
    same = (iota((256, 256), 0) & 15) == (iota((256, 256), 1) & 15)
    side_h[...], side_l[...] = select(same, [(f, column) for f in spread])
    back_h[...], back_l[...] = select(same, [(column, f) for f in spread])


def last_matrices(mixing, mix_h, mix_l, back0, back1, back2):
    parts, _, spread = spread_factor(mixing)
    tiled = one_hot((iota((256, CH), 0) & 15) == iota((256, CH), 1))
    col = iota((256, 256), 1)
    there = (iota((256, 256), 0) & 15) == 2 * ((col & 127) >> 4) + (col >> 7)
    mix_h[...], mix_l[...] = select(there, [(f, tiled) for f in spread])
    for ref, rows in ((back0, 2), (back1, 4), (back2, 8)):
        n = CH * rows
        one = one_hot(iota((n, CH), 0) // rows == iota((n, CH), 1))
        full = [dot(one, stack([f] * rows), NT) for f in parts]
        ref[...] = jnp.where(iota((n, n), 0) % rows == iota((n, n), 1) // CH, full[0] + full[1], 0.0)


def inner_kernel(grid):
    def body(weights, factor, mixing, cot, e0, e1, e2, g0, g1, g2, u0, u1, u2, h1, l1, h2, l2, h3, l3, *rest):
        *mixes, halves = rest
        ty, tx = places()
        side_matrices(mixing, *mixes)
        store_matrix(matrix_3(weights), h3, l3)
        store_matrix(matrix_2(weights), h2, l2)
        store_matrix(matrix_1(weights), h1, l1)
        for r in range(2):
            g0[r] = roll(widen(e0[:, r, :]), BASE[0])
        for r, row in enumerate(factor_rows([widen(e1[:, r, :]) for r in range(4)], factor, 1, False)):
            g1[r] = row
        for r, row in enumerate(factor_rows([e2[:, r, :] for r in range(8)], factor, 2, False)):
            g2[r] = row
        for j in (0, 1):
            halves[j] = cot[:, :, 128 * j : 128 * (j + 1)].reshape(256, 128)
        left = beside(
            [
                stack([halves[j, pl.ds(2 * i + a, CH, stride=16), :] for i in range(8)])
                for a in (0, 1)
                for j in (0, 1)
            ]
        )
        out = mul3(split(left), (h3[...], l3[...]), NT)
        up2 = block_sum(out, 8, tile)
        side2 = block_sum(tile(out, 3), 8, lambda x, da: roll(x, -4 * da))
        top = inside_mask(HALO[2], tx, grid[1] - 1, False)
        ones = jnp.ones((1, 128), F32)
        up2 = clear_outside(up2, 1, ones, ty, grid[0] - 1)
        side2 = clear_outside(side2, 1, top, ty, grid[0] - 1)
        for r, row in enumerate(up2):
            u2[r] = row
        none = [jnp.zeros((CH, 128), F32)]
        up2, side2 = none + up2 + none, none + side2 + none
        left = beside(
            [stack(up2[0::2]), stack(up2[1::2]), stack(side2[0::2]) + roll(stack(side2[1::2]), 4)]
        )
        up1 = block_sum(mul3(split(left), (h2[...], l2[...]), NT), 6, tile)
        up1 = clear_outside(up1, 2, inside_mask(HALO[1], tx, grid[1] - 1, True), ty, grid[0] - 1)
        for r, row in enumerate(up1):
            u1[r] = row
        left = beside([stack(up1[0::2]), stack(up1[1::2])])
        up0 = block_sum(mul3(split(left), (h1[...], l1[...]), NT), 4, tile)
        for r, row in enumerate(up0):
            u0[r] = row

    return body


def second_kernel(grid):
    def body(got_a, got_b, g0, g1, g2, u0, u1, u2, send_a, send_b, x0, x1, s2, v0, v1, v2):
        ty, tx = places()
        lane = iota((CH, 128), 1)
        even = (tx & 1) == 0
        k = 0
        left, right, halo = [], [], []
        for j in (0, 1):
            first, second = got_a[j], got_b[j]
            right.append(jnp.where(even, first, second))
            left.append(jnp.where(even, second, first))
            halo.append(jnp.where((lane & 3) < 2, roll(left[j], -2), roll(right[j], 2)))

        def move(parts, k, offset, target, count):
            moved = roll(parts[k // 32], target - 4 * (k % 32) - offset)
            return jnp.where((lane >= target) & (lane < target + count), moved, 0.0)

        gs = []
        for level, ref in ((0, g0), (1, g1), (2, g2)):
            rows = []
            for r in range(ROWS[level]):
                side = move(halo, k, 0, HALO[level], 4)
                rows.append((ref[r], side) if level == 2 else ref[r] + side)
                k += 1
            gs.append(rows)
        us = []
        for level, ref in ((0, u0), (1, u1), (2, u2)):
            rows = []
            for r in range(ref.shape[0]):
                row = ref[r] + move(left, k, 2, BASE[level], 2)
                rows.append(row + move(right, k, 0, BASE[level] + COLS[level] - 2, 2))
                k += 1
            us.append(rows)

        inner0 = (lane >= BASE[0]) & (lane < BASE[0] + COLS[0])

        def payload(ends, ups):
            g = [[level[e] for e in ends] for level in gs]
            tiles = [row[0] for row in g[2]]
            tiles += [one + zero + two[1] for zero, one, two in zip(*g)]
            tiles.append(us[2][-ups])
            tiles += [
                jnp.where(inner0, us[0][e], us[1][e]) for e in ends
            ]
            return tiles

        low, high = payload((0, 1), 0), payload((-2, -1), 1)
        even = (ty & 1) == 0
        for j in range(len(low)):
            send_a[j] = jnp.where(even, high[j], low[j])
            send_b[j] = jnp.where(even, low[j], high[j])
        for ref, rows in ((x0, gs[0]), (x1, gs[1]), (s2, [row[1] for row in gs[2]])):
            for j, row in enumerate(rows):
                ref[j] = row
        for ref, rows, trim in ((v0, us[0], 2), (v1, us[1], 2), (v2, us[2], 1)):
            for j in range(ref.shape[0]):
                ref[j] = rows[j + trim]

    return body


def third_kernel(grid):
    def body(factor, got_a, got_b, x0, x1, g2, s2, v0, v1, v2, local, grad, h1, l1, h2, l2, h3, l3, mix_h, mix_l, back0, back1, back2, sky, d0, d1, d2, d3):
        ty, tx = places()
        even = (ty & 1) == 0
        above, below = [], []
        for j in range(7):
            first, second = got_a[j], got_b[j]
            above.append(jnp.where(even, second, first))
            below.append(jnp.where(even, first, second))

        def trio(rows):
            return beside([stack(rows[da : da + len(rows) - 2]) for da in (0, 1, 2)])

        field = above[2:4] + [x0[r] for r in range(2)] + below[2:4]
        out = mul3(split(trio(field)), (h1[...], l1[...]), NN)
        mixed = above[2:4] + [x1[r] for r in range(4)] + below[2:4]
        field = [tile(out[CH * i : CH * (i + 1)], a) for i in range(4) for a in (0, 1)]
        field = [f + m for f, m in zip(field, mixed)]
        mask = inside_mask(HALO[1], tx, grid[1] - 1, True)
        field = clear_outside(field, 2, mask, ty, grid[0] - 1)
        out = mul3(split(trio(field)), (h2[...], l2[...]), NN)
        mixed = above[0:2] + [g2[r] for r in range(8)] + below[0:2]
        side = above[2:4] + [s2[r] for r in range(8)] + below[2:4]
        pairs = [(out[CH * i : CH * (i + 1)], a) for i in range(6) for a in (0, 1)]
        field = [tile(o, a) + m for (o, a), m in zip(pairs, mixed)]
        side = [roll(tile(o, 2), -4 * a) + m for (o, a), m in zip(pairs, side)]
        field = clear_outside(field, 2, jnp.ones((1, 128), F32), ty, grid[0] - 1)[1:11]
        mask = inside_mask(HALO[2], tx, grid[1] - 1, False)
        side = clear_outside(side, 2, mask, ty, grid[0] - 1)[1:11]
        sides = [side[i] + roll(side[i + 1], 4) + roll(side[i + 2], 8) for i in range(8)]
        out = mul3(split(beside([trio(field), stack(sides)])), (h3[...], l3[...]), NN)
        fine = split(stack([out[:, :256], out[:, 256:]]))
        sky[...] = (mul3((mix_h[...], mix_l[...]), fine, NN) + local[...]).reshape(CH, 16, 256)

        up0 = [v0[r] + above[5 + r] + below[5 + r] for r in range(2)]
        up1 = [v1[0] + above[5], v1[1] + above[6], v1[2] + below[5], v1[3] + below[6]]
        up2 = [v2[0] + above[4]] + [v2[r] for r in range(1, 7)] + [v2[7] + below[4]]
        up1 = factor_rows(up1, factor, 1, True)
        up2 = factor_rows(up2, factor, 2, True)
        for ref, rows, back, level in ((d0, up0, back0, 0), (d1, up1, back1, 1), (d2, up2, back2, 2)):
            out = mul(back[...], stack(rows))
            cols = COLS[level]
            if BASE[level]:
                out = roll(out, -BASE[level])
            out = out.reshape(CH, ROWS[level], 128)
            ref[...] = out[:, :, :cols] if cols < 128 else out
        d3[...] = grad[...]

    return body


def local_body(factor, mixing, cot, e3, side_h, side_l, back_h, back_l, local, grad, *mixes):
    last_matrices(mixing, *mixes)

    def factored(ref, transposed):
        halves = [
            factor_tile(ref[:, :, 128 * h : 128 * (h + 1)].reshape(32, 8, 128), factor, transposed).reshape(256, 128)
            for h in (0, 1)
        ]
        return split(beside(halves))

    grad[...] = mul3((back_h[...], back_l[...]), factored(cot, True), NN).reshape(CH, 16, 256)
    local[...] = mul3((side_h[...], side_l[...]), factored(e3, False), NN)


def swaps(count, first):
    pairs = []
    for i in range(first, count - 1, 2):
        pairs += [(i, i + 1), (i + 1, i)]
    return pairs


def shaped(*shape, dtype=F32):
    return jax.ShapeDtypeStruct(shape, dtype)


SMEM = pl.BlockSpec(memory_space=pltpu.SMEM)
VMEM = pl.BlockSpec(memory_space=pltpu.VMEM)
HBM = pl.BlockSpec(memory_space=pltpu.HBM)


def call(body, specs, outs, args, scratch=(), limit=VMEM_LIMIT, into=None):
    return pl.pallas_call(
        body,
        out_shape=outs,
        in_specs=specs,
        out_specs=[HBM if k == into else VMEM for k in range(len(outs))],
        scratch_shapes=list(scratch),
        compiler_params=pltpu.CompilerParams(vmem_limit_bytes=limit),
    )(*args)


def device_body(grid):
    def on_device(e0, e1, e2, e3, weights, factor, mixing, cot):
        rows = [shaped(2, CH, 128), shaped(4, CH, 128), shaped(8, CH, 128)]
        ups = [shaped(6, CH, 128), shaped(8, CH, 128), shaped(10, CH, 128)]
        (send,) = call(
            first_kernel(grid),
            [HBM] * 6,
            [shaped(2, CH, 128)],
            (weights, factor, cot, e0, e1, e2),
            [
                pltpu.SMEM((3, 4, 9), F32),
                pltpu.SMEM((3, 4, 4), F32),
                pltpu.VMEM((CH, 16, 256), F32),
                pltpu.VMEM((CH, 2, 32), F32),
                pltpu.VMEM((CH, 4, 64), F32),
                pltpu.VMEM((CH, 8, 128), F32),
                pltpu.VMEM((256, 128), F32),
                pltpu.SemaphoreType.DMA((9,)),
            ],
            60 * 1024 * 1024,
        )
        got_a = lax.ppermute(send, "tx", swaps(grid[1], 0))
        got_b = lax.ppermute(send, "tx", swaps(grid[1], 1))
        sizes = [(384, 256), (384, 384), (512, 512)]
        inner = call(
            inner_kernel(grid),
            [SMEM] * 2 + [VMEM] * 5,
            rows
            + ups
            + [shaped(*size, dtype=BF16) for size in sizes for _ in (0, 1)]
            + [shaped(256, 256, dtype=BF16)] * 4,
            (weights, factor, mixing, cot, e0, e1, e2),
            [pltpu.VMEM((2, 256, 128), F32)],
        )
        matrices, sides = inner[6:12], inner[12:]
        second = call(
            second_kernel(grid),
            [VMEM] * 8,
            [shaped(7, CH, 128)] * 2 + rows + rows,
            (got_a, got_b, *inner[:6]),
        )
        local, grad, *mixes = call(
            local_body,
            [SMEM] + [VMEM] * 7,
            [shaped(256, 256), shaped(CH, 16, 256)]
            + [shaped(256, 256, dtype=BF16)] * 2
            + [shaped(32, 32), shaped(64, 64), shaped(128, 128)],
            (factor, mixing, cot, e3, *sides),
        )
        got_a = lax.ppermute(second[0], "ty", swaps(grid[0], 0))
        got_b = lax.ppermute(second[1], "ty", swaps(grid[0], 1))
        x0, x1, s2, v0, v1, v2 = second[2:]
        sky, grad0, grad1, grad2, grad3 = call(
            third_kernel(grid),
            [SMEM] + [VMEM] * 22,
            [shaped(CH, 16, 256), shaped(CH, 2, 32), shaped(CH, 4, 64), shaped(CH, 8, 128), shaped(CH, 16, 256)],
            (factor, got_a, got_b, x0, x1, inner[2], s2, v0, v1, v2, local, grad, *matrices, *mixes),
        )
        return (sky, grad0, grad1, grad2, grad3)

    return on_device


def solution(mesh):
    tiles = P(None, "ty", "tx")
    return jax.shard_map(
        device_body((mesh.shape["ty"], mesh.shape["tx"])),
        mesh=mesh,
        in_specs=(tiles, tiles, tiles, tiles, P(), P(), P(), tiles),
        out_specs=(tiles,) * 5,
        check_vma=False,
    )
```

```python
import jax
import jax.numpy as jnp
from jax import lax
from jax.experimental import pallas as pl
from jax.experimental.pallas import tpu as pltpu
from jax.sharding import PartitionSpec as P

F32 = jnp.float32
BF16 = jnp.bfloat16
CH = 16
COLS = (32, 64, 128, 256)
ROWS = (2, 4, 8, 16)
BASE = (64, 0, 0, 0)
HALO = (96, 100, 104)
VMEM_LIMIT = 40 * 1024 * 1024


def iota(shape, dim):
    return lax.broadcasted_iota(jnp.int32, shape, dim)


def dot(left, right, dims, precision=None):
    return lax.dot_general(
        left, right, (dims, ((), ())), precision=precision, preferred_element_type=F32
    )


NN = ((1,), (0,))
NT = ((1,), (1,))


def mul(left, right):
    return dot(left, right, NN, lax.Precision.HIGHEST)


def mul_t(left, right):
    return dot(left, right, NT, lax.Precision.HIGHEST)


def split(x):
    high = x.astype(BF16)
    return high, (x - high.astype(F32)).astype(BF16)


def mul3(left, right, dims):
    return (
        dot(left[0], right[0], dims) + (dot(left[1], right[0], dims) + dot(left[0], right[1], dims))
    )


def roll(x, shift):
    shift %= 128
    return pltpu.roll(x, shift, 1) if shift else x


def places():
    return lax.axis_index("ty"), lax.axis_index("tx")


def refine_weight(weights, level, fine_col, coarse_col, a, da, along):
    step = coarse_col - (fine_col >> 1)
    odd = iota((1, 8, step.shape[2]), along) & 1
    block = jnp.zeros(step.shape, F32)
    for db in (0, 1, 2):
        n = 3 * da + db
        pair = jnp.where(odd == 0, weights[level - 1, 2 * a, n], weights[level - 1, 2 * a + 1, n])
        block = jnp.where(step == db - 1, pair, block)
    return block.reshape(step.shape[0] * 8, step.shape[2])


def fine_index(count):
    shape = (count // 8, 8, 128)
    return iota(shape, 0) * 8 + iota(shape, 1)


def lane_index(count):
    return iota((count // 8, 8, 128), 2)


def interior_col(lane, level, none):
    cols, base = COLS[level], BASE[level]
    return jnp.where((lane >= base) & (lane < base + cols), lane - base, none)


def halo_col(lane, level, place, none):
    step = lane - place
    return jnp.where(
        (step >= 0) & (step < 4), jnp.where(step < 2, step - 2, step - 2 + COLS[level]), none
    )


def both_col(lane, level, none):
    return interior_col(lane, level, halo_col(lane, level, HALO[level], none))


FAR, NEAR = -4096, 4096


def zeros(count):
    return jnp.zeros((count, 128), F32)


def lane_range(start, count):
    return iota((1, 8, count), 2) + start


def sublane_range(start, groups):
    return iota((groups, 8, 128), 0) * 8 + iota((groups, 8, 128), 1) + start


def matrix_1(weights):
    coarse, fine = both_col(sublane_range(BASE[0], 5), 0, NEAR), both_col(lane_range(0, 128), 1, FAR)
    rows = []
    for da in (0, 1, 2):
        row = []
        for a in (0, 1):
            block = refine_weight(weights, 1, fine, coarse, a, da, 2)
            row.append(stack([zeros(BASE[0]), block, zeros(88 - BASE[0])]))
        rows.append(row)
    return rows


def matrix_2(weights):
    group = iota((9, 8, 128), 0)
    coarse = jnp.where(group < 8, group, HALO[1] // 8) * 8 + iota((9, 8, 128), 1)
    coarse, lane = both_col(coarse, 1, NEAR), lane_range(0, 128)
    halos = [halo_col(lane, 2, HALO[2] + 4 * a, FAR) for a in (0, 1)]
    rows = []
    for da in (0, 1, 2):
        row = [refine_weight(weights, 2, lane, coarse, a, da, 2) for a in (0, 1)]
        row.append(sum(refine_weight(weights, 2, halos[a], coarse, a, da, 2) for a in (0, 1)))
        rows.append([stack([x[:64], zeros(32), x[64:], zeros(24)]) for x in row])
    return rows


def matrix_3(weights):
    index = sublane_range(0, 16)
    halo = sublane_range(HALO[2], 2)
    rows = []
    for da in (0, 1, 2):
        rows.append(
            [refine_weight(weights, 3, lane_range(128 * h, 128), index, a, da, 2) for a in (0, 1) for h in (0, 1)]
        )
    row = []
    for a in (0, 1):
        for h in (0, 1):
            block = sum(
                refine_weight(
                    weights, 3, lane_range(128 * h, 128), halo_col(halo, 2, HALO[2] + 4 * da, NEAR), a, da, 2
                )
                for da in (0, 1, 2)
            )
            row.append(stack([zeros(HALO[2]), block, zeros(112 - HALO[2])]))
    rows.append(row)
    return rows


def store_matrix(blocks, high_ref, low_ref):
    down = 0
    for row in blocks:
        for j, block in enumerate(row):
            high, low = split(block)
            high_ref[down : down + block.shape[0], 128 * j : 128 * (j + 1)] = high
            low_ref[down : down + block.shape[0], 128 * j : 128 * (j + 1)] = low
        down += row[0].shape[0]


def stack(rows):
    return jnp.concatenate(rows, axis=0)


def beside(parts):
    return jnp.concatenate(parts, axis=1)


def block_sum(out, blocks, part):
    result = []
    for i in range(-1, blocks + 1):
        total = None
        for da in (0, 1, 2):
            block = i - (da - 1)
            if 0 <= block < blocks:
                term = part(out[CH * block : CH * (block + 1)], da)
                total = term if total is None else total + term
        result.append(total)
    return result


def tile(x, j):
    return x[:, 128 * j : 128 * (j + 1)]


def swap_lanes(x):
    axis = x.ndim - 1
    lane = iota(x.shape, axis)
    return jnp.where((lane & 1) == 0, pltpu.roll(x, x.shape[axis] - 1, axis), pltpu.roll(x, 1, axis))


def factor_rows(rows, factor, level, transposed):
    odd = iota(rows[0].shape, 1) & 1
    swapped = [swap_lanes(r) for r in rows]

    def entry(a, b, a2, b2):
        if transposed:
            return factor[level - 1, 2 * a2 + b2, 2 * a + b]
        return factor[level - 1, 2 * a + b, 2 * a2 + b2]

    pairs = {}
    for a in (0, 1):
        for a2 in (0, 1):
            pairs[a, a2] = (
                jnp.where(odd == 0, entry(a, 0, a2, 0), entry(a, 1, a2, 1)),
                jnp.where(odd == 0, entry(a, 0, a2, 1), entry(a, 1, a2, 0)),
            )
    result = []
    for i in range(len(rows) // 2):
        for a in (0, 1):
            total = None
            for a2 in (0, 1):
                same, other = pairs[a, a2]
                term = same * rows[2 * i + a2] + other * swapped[2 * i + a2]
                total = term if total is None else total + term
            result.append(total)
    return result


def factor_tile(x, factor, transposed):
    odd_row = iota((1, 8, 128), 1) & 1
    odd_col = iota((1, 8, 128), 2) & 1
    side = swap_lanes(x)

    def swap_rows(y):
        row = iota(y.shape, 1)
        return jnp.where((row & 1) == 0, pltpu.roll(y, 7, 1), pltpu.roll(y, 1, 1))

    def coefficient(flip_row, flip_col):
        values = []
        for a in (0, 1):
            for b in (0, 1):
                here, there = 2 * (a ^ flip_row) + b, 2 * a + (b ^ flip_col)
                values.append(factor[2, there, here] if transposed else factor[2, here, there])
        return jnp.where(
            odd_row == 0,
            jnp.where(odd_col == 0, values[0], values[1]),
            jnp.where(odd_col == 0, values[2], values[3]),
        )

    return (
        coefficient(0, 0) * x
        + coefficient(0, 1) * side
        + swap_rows(coefficient(1, 0) * x + coefficient(1, 1) * side)
    )


def inside_mask(place, tx, last, keep_rest):
    lane = iota((1, 128), 1) - place
    left = jnp.where(tx == 0, 0.0, 1.0)
    right = jnp.where(tx == last, 0.0, 1.0)
    rest = jnp.full((1, 128), 1.0 if keep_rest else 0.0, F32)
    return jnp.where((lane >= 0) & (lane < 2), left, jnp.where((lane >= 2) & (lane < 4), right, rest))


def clear_outside(rows, around, mask, ty, last):
    top = jnp.where(ty == 0, 0.0, 1.0)
    bottom = jnp.where(ty == last, 0.0, 1.0)
    result = []
    for k, row in enumerate(rows):
        if k < around:
            row = row * (mask * top)
        elif k >= len(rows) - around:
            row = row * (mask * bottom)
        else:
            row = row * mask
        result.append(row)
    return result


def edge_col(lane, level, none):
    inside = (0, 2, 6, 16)[level]
    cols = COLS[level]
    if level == 3:
        return jnp.where(lane < 16, lane, jnp.where(lane < 32, cols + lane - 32, none))
    col = jnp.where(lane < 2, lane - 2, jnp.where(lane < 4, cols + lane - 2, none))
    col = jnp.where((lane >= 4) & (lane < 4 + inside), lane - 4, col)
    return jnp.where(
        (lane >= 4 + inside) & (lane < 4 + 2 * inside), cols - inside + lane - 4 - inside, col
    )


def edge_matrix(weights, level, width):
    fine = edge_col(fine_index(width), level, FAR)
    coarse = edge_col(lane_index(width), level - 1, NEAR)
    return split(
        stack([beside([refine_weight(weights, level, fine, coarse, a, da, 1) for da in (0, 1, 2)]) for a in (0, 1)])
    )


def edge_pull(rows, matrix, width):
    even, odd = stack(rows[0::2]), stack(rows[1::2])
    left = jnp.where(iota(even.shape, 1) < width, even, roll(odd, width))[:, : 2 * width]
    return block_sum(mul3(split(left), matrix, NN), len(rows) // 2, tile)


def widen(x):
    if x.shape[1] == 128:
        return x
    return beside([x, jnp.zeros((x.shape[0], 128 - x.shape[1]), F32)])


def first_kernel(grid):
    def body(weights_in, factor_in, cot_in, e0_in, e1_in, e2_in, send, weights, factor, cot, e0, e1, e2, edge, sems):
        copies = [
            pltpu.make_async_copy(source, target, sems.at[k])
            for k, (source, target) in enumerate(
                ((weights_in, weights), (factor_in, factor), (e0_in, e0), (e1_in, e1), (e2_in, e2))
            )
        ]
        for q in range(4):
            part = pl.ds(4 * q, 4)
            copies.append(pltpu.make_async_copy(cot_in.at[part], cot.at[part], sems.at[5 + q]))
        for copy in copies:
            copy.start()
        ty, tx = places()
        lane = iota((CH, 128), 1)
        for copy in copies[:5]:
            copy.wait()
        edges = [edge_matrix(weights, level, (0, 8, 16, 32)[level]) for level in (1, 2, 3)]
        for copy in copies[5:]:
            copy.wait()

        def ends(row, level):
            return jnp.where(lane < 2, row, roll(row, 4 - COLS[level]))

        pieces = [ends(widen(e0[:, r, :]), 0) for r in range(2)]
        pieces += factor_rows([ends(widen(e1[:, r, :]), 1) for r in range(4)], factor, 1, False)
        pieces += factor_rows([ends(e2[:, r, :], 2) for r in range(8)], factor, 2, False)
        low = cot[:, :, :128].reshape(256, 128)
        high = cot[:, :, 128:].reshape(256, 128)
        edge[...] = jnp.where(iota((256, 128), 1) < 16, low, roll(high, 32))
        rows = [edge[pl.ds(r, CH, stride=16), :] for r in range(16)]
        mask = inside_mask(0, tx, grid[1] - 1, True)
        up2 = clear_outside(edge_pull(rows, edges[2], 32), 1, mask, ty, grid[0] - 1)
        none = jnp.zeros((CH, 128), F32)
        up1 = edge_pull([none] + up2 + [none], edges[1], 16)
        up1 = clear_outside(up1, 2, mask, ty, grid[0] - 1)
        up0 = edge_pull(up1, edges[0], 8)
        pieces += up0 + up1 + up2
        totals = [none, none]
        for k, piece in enumerate(pieces):
            at = 4 * (k % 32)
            totals[k // 32] = jnp.where((lane >= at) & (lane < at + 4), roll(piece, at), totals[k // 32])
        send[0] = totals[0]
        send[1] = totals[1]

    return body


def one_hot(test):
    return jnp.where(test, 1.0, 0.0).astype(BF16)


def spread_factor(mixing):
    parts = split(mixing[...])
    column = one_hot(iota((256, CH), 0) // CH == iota((256, CH), 1))
    return parts, column, [dot(column, f, NN).astype(BF16) for f in parts]


def select(where, pairs):
    return [jnp.where(where, dot(x, y, NT), 0.0).astype(BF16) for x, y in pairs]


def side_matrices(mixing, side_h, side_l, back_h, back_l):
    _, column, spread = spread_factor(mixing)
    same = (iota((256, 256), 0) & 15) == (iota((256, 256), 1) & 15)
    side_h[...], side_l[...] = select(same, [(f, column) for f in spread])
    back_h[...], back_l[...] = select(same, [(column, f) for f in spread])


def last_matrices(mixing, mix_h, mix_l, back0, back1, back2):
    parts, _, spread = spread_factor(mixing)
    tiled = one_hot((iota((256, CH), 0) & 15) == iota((256, CH), 1))
    col = iota((256, 256), 1)
    there = (iota((256, 256), 0) & 15) == 2 * ((col & 127) >> 4) + (col >> 7)
    mix_h[...], mix_l[...] = select(there, [(f, tiled) for f in spread])
    for ref, rows in ((back0, 2), (back1, 4), (back2, 8)):
        n = CH * rows
        one = one_hot(iota((n, CH), 0) // rows == iota((n, CH), 1))
        full = [dot(one, stack([f] * rows), NT) for f in parts]
        ref[...] = jnp.where(iota((n, n), 0) % rows == iota((n, n), 1) // CH, full[0] + full[1], 0.0)


def inner_kernel(grid):
    def body(weights, factor, mixing, cot, e0, e1, e2, g0, g1, g2, u0, u1, u2, h1, l1, h2, l2, h3, l3, *rest):
        *mixes, halves = rest
        ty, tx = places()
        side_matrices(mixing, *mixes)
        store_matrix(matrix_3(weights), h3, l3)
        store_matrix(matrix_2(weights), h2, l2)
        store_matrix(matrix_1(weights), h1, l1)
        for r in range(2):
            g0[r] = roll(widen(e0[:, r, :]), BASE[0])
        for r, row in enumerate(factor_rows([widen(e1[:, r, :]) for r in range(4)], factor, 1, False)):
            g1[r] = row
        for r, row in enumerate(factor_rows([e2[:, r, :] for r in range(8)], factor, 2, False)):
            g2[r] = row
        for j in (0, 1):
            halves[j] = cot[:, :, 128 * j : 128 * (j + 1)].reshape(256, 128)
        left = beside(
            [
                stack([halves[j, pl.ds(2 * i + a, CH, stride=16), :] for i in range(8)])
                for a in (0, 1)
                for j in (0, 1)
            ]
        )
        out = mul3(split(left), (h3[...], l3[...]), NT)
        up2 = block_sum(out, 8, tile)
        side2 = block_sum(tile(out, 3), 8, lambda x, da: roll(x, -4 * da))
        top = inside_mask(HALO[2], tx, grid[1] - 1, False)
        ones = jnp.ones((1, 128), F32)
        up2 = clear_outside(up2, 1, ones, ty, grid[0] - 1)
        side2 = clear_outside(side2, 1, top, ty, grid[0] - 1)
        for r, row in enumerate(up2):
            u2[r] = row
        none = [jnp.zeros((CH, 128), F32)]
        up2, side2 = none + up2 + none, none + side2 + none
        left = beside(
            [stack(up2[0::2]), stack(up2[1::2]), stack(side2[0::2]) + roll(stack(side2[1::2]), 4)]
        )
        up1 = block_sum(mul3(split(left), (h2[...], l2[...]), NT), 6, tile)
        up1 = clear_outside(up1, 2, inside_mask(HALO[1], tx, grid[1] - 1, True), ty, grid[0] - 1)
        for r, row in enumerate(up1):
            u1[r] = row
        left = beside([stack(up1[0::2]), stack(up1[1::2])])
        up0 = block_sum(mul3(split(left), (h1[...], l1[...]), NT), 4, tile)
        for r, row in enumerate(up0):
            u0[r] = row

    return body


def second_kernel(grid):
    def body(got_a, got_b, g0, g1, g2, u0, u1, u2, send_a, send_b, x0, x1, s2, v0, v1, v2):
        ty, tx = places()
        lane = iota((CH, 128), 1)
        even = (tx & 1) == 0
        k = 0
        left, right, halo = [], [], []
        for j in (0, 1):
            first, second = got_a[j], got_b[j]
            right.append(jnp.where(even, first, second))
            left.append(jnp.where(even, second, first))
            halo.append(jnp.where((lane & 3) < 2, roll(left[j], -2), roll(right[j], 2)))

        def move(parts, k, offset, target, count):
            moved = roll(parts[k // 32], target - 4 * (k % 32) - offset)
            return jnp.where((lane >= target) & (lane < target + count), moved, 0.0)

        gs = []
        for level, ref in ((0, g0), (1, g1), (2, g2)):
            rows = []
            for r in range(ROWS[level]):
                side = move(halo, k, 0, HALO[level], 4)
                rows.append((ref[r], side) if level == 2 else ref[r] + side)
                k += 1
            gs.append(rows)
        us = []
        for level, ref in ((0, u0), (1, u1), (2, u2)):
            rows = []
            for r in range(ref.shape[0]):
                row = ref[r] + move(left, k, 2, BASE[level], 2)
                rows.append(row + move(right, k, 0, BASE[level] + COLS[level] - 2, 2))
                k += 1
            us.append(rows)

        inner0 = (lane >= BASE[0]) & (lane < BASE[0] + COLS[0])

        def payload(ends, ups):
            g = [[level[e] for e in ends] for level in gs]
            tiles = [row[0] for row in g[2]]
            tiles += [one + zero + two[1] for zero, one, two in zip(*g)]
            tiles.append(us[2][-ups])
            tiles += [
                jnp.where(inner0, us[0][e], us[1][e]) for e in ends
            ]
            return tiles

        low, high = payload((0, 1), 0), payload((-2, -1), 1)
        even = (ty & 1) == 0
        for j in range(len(low)):
            send_a[j] = jnp.where(even, high[j], low[j])
            send_b[j] = jnp.where(even, low[j], high[j])
        for ref, rows in ((x0, gs[0]), (x1, gs[1]), (s2, [row[1] for row in gs[2]])):
            for j, row in enumerate(rows):
                ref[j] = row
        for ref, rows, trim in ((v0, us[0], 2), (v1, us[1], 2), (v2, us[2], 1)):
            for j in range(ref.shape[0]):
                ref[j] = rows[j + trim]

    return body


def third_kernel(grid):
    def body(factor, got_a, got_b, x0, x1, g2, s2, v0, v1, v2, local, grad, h1, l1, h2, l2, h3, l3, mix_h, mix_l, back0, back1, back2, sky, d0, d1, d2, d3):
        ty, tx = places()
        even = (ty & 1) == 0
        above, below = [], []
        for j in range(7):
            first, second = got_a[j], got_b[j]
            above.append(jnp.where(even, second, first))
            below.append(jnp.where(even, first, second))

        def trio(rows):
            return beside([stack(rows[da : da + len(rows) - 2]) for da in (0, 1, 2)])

        field = above[2:4] + [x0[r] for r in range(2)] + below[2:4]
        out = mul3(split(trio(field)), (h1[...], l1[...]), NN)
        mixed = above[2:4] + [x1[r] for r in range(4)] + below[2:4]
        field = [tile(out[CH * i : CH * (i + 1)], a) for i in range(4) for a in (0, 1)]
        field = [f + m for f, m in zip(field, mixed)]
        mask = inside_mask(HALO[1], tx, grid[1] - 1, True)
        field = clear_outside(field, 2, mask, ty, grid[0] - 1)
        out = mul3(split(trio(field)), (h2[...], l2[...]), NN)
        mixed = above[0:2] + [g2[r] for r in range(8)] + below[0:2]
        side = above[2:4] + [s2[r] for r in range(8)] + below[2:4]
        pairs = [(out[CH * i : CH * (i + 1)], a) for i in range(6) for a in (0, 1)]
        field = [tile(o, a) + m for (o, a), m in zip(pairs, mixed)]
        side = [roll(tile(o, 2), -4 * a) + m for (o, a), m in zip(pairs, side)]
        field = clear_outside(field, 2, jnp.ones((1, 128), F32), ty, grid[0] - 1)[1:11]
        mask = inside_mask(HALO[2], tx, grid[1] - 1, False)
        side = clear_outside(side, 2, mask, ty, grid[0] - 1)[1:11]
        sides = [side[i] + roll(side[i + 1], 4) + roll(side[i + 2], 8) for i in range(8)]
        out = mul3(split(beside([trio(field), stack(sides)])), (h3[...], l3[...]), NN)
        fine = split(stack([out[:, :256], out[:, 256:]]))
        sky[...] = (mul3((mix_h[...], mix_l[...]), fine, NN) + local[...]).reshape(CH, 16, 256)

        up0 = [v0[r] + above[5 + r] + below[5 + r] for r in range(2)]
        up1 = [v1[0] + above[5], v1[1] + above[6], v1[2] + below[5], v1[3] + below[6]]
        up2 = [v2[0] + above[4]] + [v2[r] for r in range(1, 7)] + [v2[7] + below[4]]
        up1 = factor_rows(up1, factor, 1, True)
        up2 = factor_rows(up2, factor, 2, True)
        for ref, rows, back, level in ((d0, up0, back0, 0), (d1, up1, back1, 1), (d2, up2, back2, 2)):
            out = mul(back[...], stack(rows))
            cols = COLS[level]
            if BASE[level]:
                out = roll(out, -BASE[level])
            out = out.reshape(CH, ROWS[level], 128)
            ref[...] = out[:, :, :cols] if cols < 128 else out
        d3[...] = grad[...]

    return body


def local_body(factor, mixing, cot, e3, side_h, side_l, back_h, back_l, local, grad, *mixes):
    last_matrices(mixing, *mixes)

    def factored(ref, transposed):
        halves = [
            factor_tile(ref[:, :, 128 * h : 128 * (h + 1)].reshape(32, 8, 128), factor, transposed).reshape(256, 128)
            for h in (0, 1)
        ]
        return split(beside(halves))

    grad[...] = mul3((back_h[...], back_l[...]), factored(cot, True), NN).reshape(CH, 16, 256)
    local[...] = mul3((side_h[...], side_l[...]), factored(e3, False), NN)


def swaps(count, first):
    pairs = []
    for i in range(first, count - 1, 2):
        pairs += [(i, i + 1), (i + 1, i)]
    return pairs


def shaped(*shape, dtype=F32):
    return jax.ShapeDtypeStruct(shape, dtype)


SMEM = pl.BlockSpec(memory_space=pltpu.SMEM)
VMEM = pl.BlockSpec(memory_space=pltpu.VMEM)
HBM = pl.BlockSpec(memory_space=pltpu.HBM)


def call(body, specs, outs, args, scratch=(), limit=VMEM_LIMIT, into=None):
    return pl.pallas_call(
        body,
        out_shape=outs,
        in_specs=specs,
        out_specs=[HBM if k == into else VMEM for k in range(len(outs))],
        scratch_shapes=list(scratch),
        compiler_params=pltpu.CompilerParams(vmem_limit_bytes=limit),
    )(*args)


def device_body(grid):
    def on_device(e0, e1, e2, e3, weights, factor, mixing, cot):
        rows = [shaped(2, CH, 128), shaped(4, CH, 128), shaped(8, CH, 128)]
        ups = [shaped(6, CH, 128), shaped(8, CH, 128), shaped(10, CH, 128)]
        (send,) = call(
            first_kernel(grid),
            [HBM] * 6,
            [shaped(2, CH, 128)],
            (weights, factor, cot, e0, e1, e2),
            [
                pltpu.SMEM((3, 4, 9), F32),
                pltpu.SMEM((3, 4, 4), F32),
                pltpu.VMEM((CH, 16, 256), F32),
                pltpu.VMEM((CH, 2, 32), F32),
                pltpu.VMEM((CH, 4, 64), F32),
                pltpu.VMEM((CH, 8, 128), F32),
                pltpu.VMEM((256, 128), F32),
                pltpu.SemaphoreType.DMA((9,)),
            ],
            60 * 1024 * 1024,
        )
        got_a = lax.ppermute(send, "tx", swaps(grid[1], 0))
        got_b = lax.ppermute(send, "tx", swaps(grid[1], 1))
        sizes = [(384, 256), (384, 384), (512, 512)]
        inner = call(
            inner_kernel(grid),
            [SMEM] * 2 + [VMEM] * 5,
            rows
            + ups
            + [shaped(*size, dtype=BF16) for size in sizes for _ in (0, 1)]
            + [shaped(256, 256, dtype=BF16)] * 4,
            (weights, factor, mixing, cot, e0, e1, e2),
            [pltpu.VMEM((2, 256, 128), F32)],
        )
        matrices, sides = inner[6:12], inner[12:]
        second = call(
            second_kernel(grid),
            [VMEM] * 8,
            [shaped(7, CH, 128)] * 2 + rows + rows,
            (got_a, got_b, *inner[:6]),
        )
        local, grad, *mixes = call(
            local_body,
            [SMEM] + [VMEM] * 7,
            [shaped(256, 256), shaped(CH, 16, 256)]
            + [shaped(256, 256, dtype=BF16)] * 2
            + [shaped(32, 32), shaped(64, 64), shaped(128, 128)],
            (factor, mixing, cot, e3, *sides),
        )
        got_a = lax.ppermute(second[0], "ty", swaps(grid[0], 0))
        got_b = lax.ppermute(second[1], "ty", swaps(grid[0], 1))
        x0, x1, s2, v0, v1, v2 = second[2:]
        sky, grad0, grad1, grad2, grad3 = call(
            third_kernel(grid),
            [SMEM] + [VMEM] * 22,
            [shaped(CH, 16, 256), shaped(CH, 2, 32), shaped(CH, 4, 64), shaped(CH, 8, 128), shaped(CH, 16, 256)],
            (factor, got_a, got_b, x0, x1, inner[2], s2, v0, v1, v2, local, grad, *matrices, *mixes),
        )
        return (sky, grad0, grad1, grad2, grad3)

    return on_device


def solution(mesh):
    tiles = P(None, "ty", "tx")
    return jax.shard_map(
        device_body((mesh.shape["ty"], mesh.shape["tx"])),
        mesh=mesh,
        in_specs=(tiles, tiles, tiles, tiles, P(), P(), P(), tiles),
        out_specs=(tiles,) * 5,
        check_vma=False,
    )
```
